128 devices in a mesh: grp: 4 (over z), dev: 32 (over x, y, core).
Axes of the slice: x: 4, y: 4, z: 4, core: 2. Of those that a mesh axis runs over, the one named last changes fastest.
Arguments:
- a_blocks: bfloat16 [16384, 64, 512], P(('grp', 'dev')), may hold values from -0.25 to 0.25
- a_cols: int32 [16384, 8], P(('grp', 'dev')), may hold values from 0 to 16383, as said below
- p_blocks: bfloat16 [16384, 64, 256], P(('grp', 'dev')), may hold values from -0.75 to 0.75
- ap_slots: int32 [16384, 32], P(('grp', 'dev')), may hold values from 0 to 7
- p_touch: int32 [16384, 4], P(('grp', 'dev')), may hold values from 0 to 223
- owner_dev: int32 [28672, 1], P(('grp', 'dev')), may hold values from 0 to 127, as said below
- owner_row: int32 [28672], P(('grp', 'dev')), may hold values from 0 to 7
Outputs:
- coarse: bfloat16 [1024, 64, 512], P('dev')
The draws below stay inside these ranges and needn't reach their ends.
Inputs may be any that keep to these rules, and one draw needn't show every extreme that they name: `a_cols`: entries 0 to 5 of a row name fine rows of the same device; entry 6 names one of the last 32 rows of the device before it, entry 7 one of the first 32 rows of the device after it (rows of the same device on the first and last device). `owner_dev`: the owner of a column of device q is q, q - 1 or q + 1; at most 28 of the 224 columns of one device are owned by q - 1, and at most 28 by q + 1, and some device reaches 28 on each side.
All inputs are finite; a program needn't handle non-finite values.
Results may differ from the reference program's by a relative error of at most 0.006.
Values may be sent and summed in bfloat16 or wider, within the bound.
A program may use at most 256 MiB of HBM per device.

```python
import jax
import jax.numpy as jnp
from jax import lax

BS = 64
FB = 128
KA = 8
KP = 4
KC = 8
CB = 8
NT = 224
CAP = 28
FINE = 16384
N_GRP = 4
N_DEV = 32


def draw_a_cols(key, part):
    key = jax.random.fold_in(key, 11)
    key_own, key_before, key_after = jax.random.split(key, 3)
    positions = jnp.arange(FINE)
    device_of = positions // FB
    count = FINE // FB
    own_rows = device_of[:, None] * FB + jax.random.randint(key_own, (FINE, KA), 0, FB)
    before = device_of * FB - 1 - jax.random.randint(key_before, (FINE,), 0, FB // 4)
    after = (device_of + 1) * FB + jax.random.randint(key_after, (FINE,), 0, FB // 4)
    before = jnp.where(device_of > 0, before, own_rows[:, KA - 2])
    after = jnp.where(device_of < count - 1, after, own_rows[:, KA - 1])
    joined = jnp.concatenate([own_rows[:, :KA - 2], before[:, None], after[:, None]], axis=1)
    return joined.astype(jnp.int32)


def draw_owner_dev(key, part):
    key = jax.random.fold_in(key, 23)
    count = FINE // FB
    key_prev, key_next, key_perm = jax.random.split(key, 3)
    lowest = max(1, CAP // 2)
    prev_count = jax.random.randint(key_prev, (count,), lowest, CAP + 1)
    next_count = jax.random.randint(key_next, (count,), lowest, CAP + 1)
    device = jnp.arange(count)
    prev_count = jnp.where(device == 1, CAP, prev_count)
    next_count = jnp.where(device == 0, CAP, next_count)
    prev_count = jnp.where(device == 0, 0, prev_count)
    next_count = jnp.where(device == count - 1, 0, next_count)
    keys = jax.random.split(key_perm, count)
    ranks = jax.vmap(lambda single: jax.random.permutation(single, NT))(keys)
    owner = jnp.where(ranks < prev_count[:, None], device[:, None] - 1, jnp.where(ranks < (prev_count + next_count)[:, None], device[:, None] + 1, device[:, None]))
    return owner.reshape(count * NT, 1).astype(jnp.int32)


def with_ends(entries, key, low, high):
    dims = entries.shape
    place = [jax.random.randint(jax.random.fold_in(key, axis), (), 0, dims[axis]) for axis in range(len(dims))]
    entries = entries.at[tuple(place)].set(low)
    longest = dims.index(max(dims))
    place[longest] = (place[longest] + 1) % dims[longest]
    return entries.at[tuple(place)].set(high)


def block_levels(rng, dims, cuts, low, top_value):
    def one(dim, parts):
        draws = jax.random.uniform(jax.random.fold_in(jax.random.fold_in(rng, 6), dim), (parts,), jnp.float32, low / len(cuts), top_value / len(cuts))
        return jnp.repeat(jnp.exp(draws), dims[dim] // parts).reshape((-1,) + (1,) * (len(dims) - dim - 1))

    level = one(*cuts[0])
    for cut in cuts[1:]:
        level = level * one(*cut)
    return level


def scatter_about(own_key, extent, width, most, shards=(), kind=jnp.bfloat16):
    drawn = jax.random.normal(own_key, extent, jnp.float32) * width
    if len(shards) > 0:
        drawn = block_levels(own_key, extent, shards, -0.22, 0.18) * drawn
    return jnp.clip(drawn, min=-most, max=most).astype(kind)


def setup_inputs(seed: int = 0) -> dict:
    splits = jax.random.split(jax.random.key(seed), 8)
    a_blocks = scatter_about(splits[0], (FINE, BS, KA * BS), (KA * BS) ** -0.5, 0.25, ((0, 128),))
    a_cols = draw_a_cols(jax.random.fold_in(splits[7], 71), 0)
    p_blocks = scatter_about(splits[2], (FINE, BS, KP * BS), BS ** -0.5, 0.75, ((0, 128),))
    ap_slots = with_ends(jax.random.randint(splits[3], (FINE, KA * KP), 0, KC), jax.random.fold_in(splits[3], 1), 0, KC - 1).astype(jnp.int32)
    p_touch = with_ends(jax.random.randint(splits[4], (FINE, KP), 0, NT), jax.random.fold_in(splits[4], 1), 0, NT - 1).astype(jnp.int32)
    owner_dev = draw_owner_dev(jax.random.fold_in(splits[7], 71), 0)
    owner_row = with_ends(jax.random.randint(splits[6], (N_GRP * N_DEV * NT,), 0, CB), jax.random.fold_in(splits[6], 1), 0, CB - 1).astype(jnp.int32)
    return dict(a_blocks=a_blocks, a_cols=a_cols, p_blocks=p_blocks, ap_slots=ap_slots, p_touch=p_touch, owner_dev=owner_dev, owner_row=owner_row)


def reference(a_blocks, a_cols, p_blocks, ap_slots, p_touch, owner_dev, owner_row):
    devices = N_GRP * N_DEV
    a_grid = a_blocks.reshape(devices, FB, BS, KA, BS)
    columns = a_cols.reshape(devices, FB, KA)
    slot_map = ap_slots.reshape(devices, FB, KA, KP)
    touched = p_touch.reshape(devices, FB, KP)
    p_grid = p_blocks.reshape(devices, FB, BS, KP, BS)
    p_flat = p_blocks.reshape(FINE, BS, KP, BS)
    targets = owner_dev.reshape(devices, NT)
    target_rows = owner_row.reshape(devices, NT)

    def accumulate(total, inputs):
        a_dev, col_dev, slot_dev, touch_dev, p_dev, dest_dev, row_dev = inputs
        nearby = p_flat[col_dev].astype(jnp.float32)
        products = jnp.einsum("iakb,ikbmc->ikmac", a_dev.astype(jnp.float32), nearby,
                              precision=lax.Precision.HIGHEST)
        onehot = (slot_dev[..., None] == jnp.arange(KC)).astype(jnp.float32)
        assembled = jnp.einsum("ikms,ikmac->iasc", onehot, products, precision=lax.Precision.HIGHEST)
        rounded = lax.optimization_barrier(assembled.reshape(FB, BS, KC * BS).astype(jnp.bfloat16))
        pieces = jnp.einsum("iamb,ian->imbn", p_dev.astype(jnp.float32), rounded.astype(jnp.float32),
                            precision=lax.Precision.HIGHEST)
        summed = jax.ops.segment_sum(pieces.reshape(FB * KP, BS, KC * BS), touch_dev.reshape(-1),
                                     num_segments=NT)
        summed = lax.optimization_barrier(summed.astype(jnp.bfloat16)).astype(jnp.float32)
        flat_rows = (dest_dev * CB + row_dev).astype(jnp.int32)
        return total.at[flat_rows].add(summed), None

    start = jnp.zeros((devices * CB, BS, KC * BS), jnp.float32)
    owned, _ = lax.scan(accumulate, start,
                        (a_grid, columns, slot_map, touched, p_grid, targets, target_rows))
    owned = owned.astype(jnp.bfloat16).reshape(N_GRP, N_DEV, CB, BS, KC * BS)
    return jnp.transpose(owned, (1, 0, 2, 3, 4)).reshape(N_DEV * N_GRP * CB, BS, KC * BS)
```

```python
import functools

import jax
import jax.numpy as jnp
from jax import lax
from jax.experimental import pallas as pl
from jax.experimental.pallas import tpu as pltpu
from jax.sharding import PartitionSpec as P

BS = 64
KA = 8
KP = 4
KC = 8
CB = 8
NT = 224
FB = 128
HALO = 32
SUBSETS = 1 << KP
WINDOW = FB + 2 * HALO
P_ROWS = 16
LOCAL_STEPS = FB // P_ROWS
HALO_STEPS = HALO // P_ROWS
BUILD_STEPS = LOCAL_STEPS + 2 * HALO_STEPS
GROUP = 8
UNROLL = 4
MAIN_STEPS = FB // GROUP
TARGETS = 3 * CB
MESH = pl.DeviceIdType.MESH


def build_rows(source, base, table, left):
    def row(r, carry):
        p = source[r].astype(jnp.float32)
        single = []
        for pair in range(KP // 2):
            tile = p[:, pair * 128:(pair + 1) * 128]
            turned = pltpu.roll(tile, 64, 1)
            single.append(jnp.where(left, tile, turned))
            single.append(jnp.where(left, turned, tile))
        sums = {0: None}
        at = (base + r) * SUBSETS
        for subset in range(1, SUBSETS):
            low = subset & -subset
            rest = subset ^ low
            value = single[low.bit_length() - 1]
            if rest:
                value = value + sums[rest]
            sums[subset] = value
            table[at + subset] = value.astype(jnp.bfloat16)
        return carry

    lax.fori_loop(0, P_ROWS, row, 0)


def galerkin_kernel(codes, touch, targets, p_local, p_prev, p_next, a_ref, p_ref, own_ref, prev_ref,
                    next_ref, table, acc):
    step = pl.program_id(0)
    left = lax.broadcasted_iota(jnp.int32, (BS, 128), 1) < 64

    @pl.when(step == 0)
    def _():
        table[0] = jnp.zeros((BS, 128), jnp.bfloat16)
        acc[...] = jnp.zeros_like(acc)

    @pl.when(step < LOCAL_STEPS)
    def _():
        build_rows(p_local, step * P_ROWS, table, left)

    @pl.when((step >= LOCAL_STEPS) & (step < LOCAL_STEPS + HALO_STEPS))
    def _():
        build_rows(p_prev, step * P_ROWS, table, left)

    @pl.when((step >= LOCAL_STEPS + HALO_STEPS) & (step < BUILD_STEPS))
    def _():
        build_rows(p_next, step * P_ROWS, table, left)

    @pl.when(step >= BUILD_STEPS)
    def _():
        first = (step - BUILD_STEPS) * GROUP

        def rows(it, carry):
            for u in range(UNROLL):
                r = it * UNROLL + u
                i = first + r
                halves = []
                for nt in range(2):
                    total = None
                    for kt in range(2):
                        blocks = []
                        for k in range(4 * kt, 4 * kt + 4):
                            tiles = []
                            for s in range(4 * nt, 4 * nt + 4, 2):
                                at = i * (KA * KC) + k * KC + s
                                tiles.append(jnp.where(left, table[codes[at]], table[codes[at + 1]]))
                            blocks.append(jnp.concatenate(tiles, axis=1))
                        part = jnp.dot(a_ref[r, :, kt * 256:(kt + 1) * 256],
                                       jnp.concatenate(blocks, axis=0),
                                       preferred_element_type=jnp.float32)
                        total = part if total is None else total + part
                    halves.append(total.astype(jnp.bfloat16))
                rounded = jnp.concatenate(halves, axis=1)
                pieces = lax.dot_general(p_ref[r], rounded, (((0,), (0,)), ((), ())),
                                         preferred_element_type=jnp.float32)
                for m in range(KP):
                    to = targets[touch[i * KP + m]]
                    acc[to] += pieces[m * BS:(m + 1) * BS]
            return carry

        lax.fori_loop(0, GROUP // UNROLL, rows, 0)

    @pl.when(step == BUILD_STEPS + MAIN_STEPS - 1)
    def _():
        prev_ref[...] = acc[0:CB].astype(jnp.bfloat16)
        own_ref[...] = acc[CB:2 * CB]
        next_ref[...] = acc[2 * CB:3 * CB].astype(jnp.bfloat16)


def galerkin(codes, touch, targets, p_local, p_prev, p_next, a_blocks):
    def clamp(value, top):
        return jnp.clip(value, 0, top)

    def main(step):
        return clamp(step - BUILD_STEPS, MAIN_STEPS - 1)

    whole = lambda s, *_: (0, 0, 0)
    p_shape = (P_ROWS, BS, KP * BS)
    grid_spec = pltpu.PrefetchScalarGridSpec(
        num_scalar_prefetch=3,
        grid=(BUILD_STEPS + MAIN_STEPS,),
        in_specs=[
            pl.BlockSpec(p_shape, lambda s, *_: (clamp(s, LOCAL_STEPS - 1), 0, 0)),
            pl.BlockSpec(p_shape, lambda s, *_: (clamp(s - LOCAL_STEPS, HALO_STEPS - 1), 0, 0)),
            pl.BlockSpec(p_shape, lambda s, *_: (clamp(s - LOCAL_STEPS - HALO_STEPS, HALO_STEPS - 1), 0, 0)),
            pl.BlockSpec((GROUP, BS, KA * BS), lambda s, *_: (main(s), 0, 0)),
            pl.BlockSpec((GROUP, BS, KP * BS), lambda s, *_: (main(s), 0, 0)),
        ],
        out_specs=[pl.BlockSpec((CB, BS, KC * BS), whole)] * 3,
        scratch_shapes=[
            pltpu.VMEM((WINDOW * SUBSETS, BS, 128), jnp.bfloat16),
            pltpu.VMEM((TARGETS, BS, KC * BS), jnp.float32),
        ],
    )
    rows = (CB, BS, KC * BS)
    return pl.pallas_call(
        galerkin_kernel,
        grid_spec=grid_spec,
        out_shape=[
            jax.ShapeDtypeStruct(rows, jnp.float32),
            jax.ShapeDtypeStruct(rows, jnp.bfloat16),
            jax.ShapeDtypeStruct(rows, jnp.bfloat16),
        ],
        compiler_params=pltpu.CompilerParams(vmem_limit_bytes=62 * 1024 * 1024),
        cost_estimate=pl.CostEstimate(flops=8_600_000_000, bytes_accessed=20_000_000, transcendentals=0),
    )(codes, touch, targets, p_local, p_prev, p_next, a_blocks, p_local)


def exchange_kernel(n_grp, n_dev, own_ref, prev_ref, next_ref, out_ref, from_prev, from_next, sems_out,
                    sems_in):
    g = lax.axis_index("grp")
    d = lax.axis_index("dev")
    count = n_grp * n_dev
    position = g * n_dev + d
    after = lax.rem(position + 1, count)
    before = lax.rem(position + count - 1, count)
    after_id = (after // n_dev, lax.rem(after, n_dev))
    before_id = (before // n_dev, lax.rem(before, n_dev))
    up_id = (lax.rem(g + 1, n_grp), d)
    down_id = (lax.rem(g + n_grp - 1, n_grp), d)

    barrier = pltpu.get_barrier_semaphore()
    for other in (after_id, before_id, up_id, down_id):
        pl.semaphore_signal(barrier, inc=1, device_id=other, device_id_type=MESH)
    pl.semaphore_wait(barrier, 4)

    def copy(source, target, kind, r, device):
        return pltpu.make_async_remote_copy(
            src_ref=source, dst_ref=target, send_sem=sems_out.at[kind, r], recv_sem=sems_in.at[kind, r],
            device_id=device, device_id_type=MESH)

    sent = []
    to_after = [copy(next_ref.at[r], from_prev.at[r], 0, r, after_id) for r in range(CB)]
    to_before = [copy(prev_ref.at[r], from_next.at[r], 1, r, before_id) for r in range(CB)]
    for r in range(CB):
        to_after[r].start()
        to_before[r].start()
    below = lax.rem(g + n_grp - 1, n_grp)
    above = lax.rem(g + 1, n_grp)
    ups, downs, relays = [], [], []

    def relay(r):
        if r < CB // 2:
            ups[r].wait_recv()
            block = below * CB + r
            onward = copy(out_ref.at[block], out_ref.at[block], 4, r, up_id)
        else:
            downs[r].wait_recv()
            block = above * CB + r
            onward = copy(out_ref.at[block], out_ref.at[block], 4, r, down_id)
        onward.start()
        relays.append(onward)

    for r in range(CB):
        to_after[r].wait_recv()
        to_before[r].wait_recv()
        total = own_ref[r] + from_prev[r].astype(jnp.float32) + from_next[r].astype(jnp.float32)
        block = g * CB + r
        out_ref[block] = total.astype(jnp.bfloat16)
        up = copy(out_ref.at[block], out_ref.at[block], 2, r, up_id)
        down = copy(out_ref.at[block], out_ref.at[block], 3, r, down_id)
        up.start()
        down.start()
        ups.append(up)
        downs.append(down)
        if r >= 1:
            relay(r - 1)
    relay(CB - 1)
    for r in range(CB):
        if r < CB // 2:
            downs[r].wait_recv()
        else:
            ups[r].wait_recv()
        relays[r].wait_recv()
        for c in (to_after[r], to_before[r], ups[r], downs[r], relays[r]):
            c.wait_send()


def exchange(own, to_prev, to_next):
    n_grp, n_dev = lax.axis_size("grp"), lax.axis_size("dev")
    rows = (CB, BS, KC * BS)
    return pl.pallas_call(
        functools.partial(exchange_kernel, n_grp, n_dev),
        out_shape=jax.ShapeDtypeStruct((n_grp * CB, BS, KC * BS), jnp.bfloat16),
        in_specs=[pl.BlockSpec(memory_space=pltpu.VMEM)] * 3,
        out_specs=pl.BlockSpec(memory_space=pltpu.VMEM),
        scratch_shapes=[
            pltpu.VMEM(rows, jnp.bfloat16),
            pltpu.VMEM(rows, jnp.bfloat16),
            pltpu.SemaphoreType.DMA((5, CB)),
            pltpu.SemaphoreType.DMA((5, CB)),
        ],
        compiler_params=pltpu.CompilerParams(collective_id=0, has_side_effects=True,
                                             vmem_limit_bytes=32 * 1024 * 1024),
    )(own, to_prev, to_next)


def on_device(a_blocks, a_cols, p_blocks, ap_slots, p_touch, owner_dev, owner_row):
    axes = ("grp", "dev")
    position = lax.axis_index(axes)
    count = lax.axis_size(axes)
    up = [(i, (i + 1) % count) for i in range(count)]
    down = [(j, i) for i, j in up]
    p_prev = lax.ppermute(p_blocks[FB - HALO:], axes, up)
    p_next = lax.ppermute(p_blocks[:HALO], axes, down)

    local = a_cols - position * FB
    window = jnp.where(local < 0, local + HALO + FB, jnp.where(local >= FB, local + HALO, local))
    slots = ap_slots.reshape(FB, KA, KP)
    weights = jnp.int32(1) << jnp.arange(KP, dtype=jnp.int32)
    hits = slots[:, :, :, None] == jnp.arange(KC, dtype=jnp.int32)
    subset = jnp.sum(jnp.where(hits, weights[:, None], 0), axis=2)
    codes = jnp.where(subset == 0, 0, window[:, :, None] * SUBSETS + subset)
    targets = (owner_dev[:, 0] - position + 1) * CB + owner_row
    own, to_prev, to_next = galerkin(codes.reshape(-1), p_touch.reshape(-1), targets, p_blocks, p_prev, p_next,
                                     a_blocks)
    return exchange(own, to_prev, to_next)


def solution(mesh):
    placed = (
        P(("grp", "dev"), None, None),
        P(("grp", "dev"), None),
        P(("grp", "dev"), None, None),
        P(("grp", "dev"), None),
        P(("grp", "dev"), None),
        P(("grp", "dev"), None),
        P(("grp", "dev")),
    )
    return jax.shard_map(
        on_device, mesh=mesh, in_specs=placed, out_specs=P("dev", None, None), check_vma=False
    )
```

```python
import functools

import jax
import jax.numpy as jnp
from jax import lax
from jax.experimental import pallas as pl
from jax.experimental.pallas import tpu as pltpu
from jax.sharding import PartitionSpec as P

BS = 64
KA = 8
KP = 4
KC = 8
CB = 8
NT = 224
FB = 128
HALO = 32
SUBSETS = 1 << KP
P_ROWS = 32
LOCAL_STEPS = FB // P_ROWS
GROUP = 16
UNROLL = 8
MAIN_STEPS = FB // GROUP
TARGETS = 3 * CB
MESH = pl.DeviceIdType.MESH


def build_rows(source, base, table, left):
    def row(r, carry):
        p = source[r].astype(jnp.float32)
        single = []
        for pair in range(KP // 2):
            tile = p[:, pair * 128:(pair + 1) * 128]
            turned = pltpu.roll(tile, 64, 1)
            single.append(jnp.where(left, tile, turned))
            single.append(jnp.where(left, turned, tile))
        sums = {0: None}
        at = (base + r) * SUBSETS
        for subset in range(1, SUBSETS):
            low = subset & -subset
            rest = subset ^ low
            value = single[low.bit_length() - 1]
            if rest:
                value = value + sums[rest]
            sums[subset] = value
            table[at + subset] = value.astype(jnp.bfloat16)
        return carry

    lax.fori_loop(0, P_ROWS, row, 0, unroll=4)


def left_half():
    return lax.broadcasted_iota(jnp.int32, (BS, 128), 1) < 64


def coefficients(table, codes, first, blocks, nt, left):
    rows = []
    for k in range(blocks):
        tiles = []
        for s in range(4 * nt, 4 * nt + 4, 2):
            at = first + k * KC + s
            tiles.append(jnp.where(left, table[codes[at]], table[codes[at + 1]]))
        rows.append(jnp.concatenate(tiles, axis=1))
    return jnp.concatenate(rows, axis=0)


def local_kernel(codes, edge, p_ref, a_ref, out_ref, table):
    step = pl.program_id(0)
    left = left_half()

    @pl.when(step == 0)
    def _():
        table[0] = jnp.zeros((BS, 128), jnp.bfloat16)

    @pl.when(step < LOCAL_STEPS)
    def _():
        build_rows(p_ref, step * P_ROWS, table, left)

    def assemble(cuts):
        first = (step - LOCAL_STEPS) * GROUP

        def rows(it, carry):
            for u in range(UNROLL):
                r = it * UNROLL + u
                for nt in range(2):
                    total = None
                    for low, high in cuts:
                        weights = coefficients(table, codes, (first + r) * (KA * KC) + low * KC, high - low, nt, left)
                        part = jnp.dot(a_ref[r, :, low * BS:high * BS], weights,
                                       preferred_element_type=jnp.float32)
                        total = part if total is None else total + part
                    out_ref[r, :, nt * 256:(nt + 1) * 256] = total.astype(jnp.bfloat16)
            return carry

        lax.fori_loop(0, GROUP // UNROLL, rows, 0)

    @pl.when((step >= LOCAL_STEPS) & (edge[0] == 0))
    def _():
        assemble(((0, 4), (4, KA - 2)))

    @pl.when((step >= LOCAL_STEPS) & (edge[0] != 0))
    def _():
        assemble(((0, 4), (4, KA)))


def local_part(codes, edge, p_local, a_blocks):
    main = lambda s, *_: (jnp.maximum(s - LOCAL_STEPS, 0), 0, 0)
    return pl.pallas_call(
        local_kernel,
        grid_spec=pltpu.PrefetchScalarGridSpec(
            num_scalar_prefetch=2,
            grid=(LOCAL_STEPS + MAIN_STEPS,),
            in_specs=[
                pl.BlockSpec((P_ROWS, BS, KP * BS), lambda s, *_: (jnp.minimum(s, LOCAL_STEPS - 1), 0, 0)),
                pl.BlockSpec((GROUP, BS, KA * BS), main),
            ],
            out_specs=pl.BlockSpec((GROUP, BS, KC * BS), main),
            scratch_shapes=[pltpu.VMEM((FB * SUBSETS, BS, 128), jnp.bfloat16)],
        ),
        out_shape=jax.ShapeDtypeStruct((FB, BS, KC * BS), jnp.bfloat16),
        compiler_params=pltpu.CompilerParams(vmem_limit_bytes=44 * 1024 * 1024),
        cost_estimate=pl.CostEstimate(flops=16_000_000_000, bytes_accessed=20_000_000, transcendentals=0),
    )(codes, edge, p_local, a_blocks)


def halo_kernel(codes, touch, targets, p_prev, p_next, part_ref, a_ref, p_ref, own_ref, prev_ref, next_ref,
                table, acc):
    step = pl.program_id(0)
    left = left_half()

    @pl.when(step == 0)
    def _():
        acc[...] = jnp.zeros_like(acc)
        build_rows(p_prev, 0, table, left)
        build_rows(p_next, HALO, table, left)
        table[0] = jnp.zeros((BS, 128), jnp.bfloat16)

    def rows(it, carry):
        kept = []
        for u in range(UNROLL + 1):
            if u < UNROLL:
                r = it * UNROLL + u
                i = step * GROUP + r
                halves = []
                for nt in range(2):
                    weights = coefficients(table, codes, i * (2 * KC), 2, nt, left)
                    total = jnp.dot(a_ref[r], weights, preferred_element_type=jnp.float32)
                    total = total + part_ref[r, :, nt * 256:(nt + 1) * 256].astype(jnp.float32)
                    halves.append(total.astype(jnp.bfloat16))
                kept.append(jnp.concatenate(halves, axis=1))
            if u >= 1:
                r = it * UNROLL + u - 1
                i = step * GROUP + r
                pieces = lax.dot_general(p_ref[r], kept[u - 1], (((0,), (0,)), ((), ())),
                                         preferred_element_type=jnp.float32)
                for m in range(KP):
                    to = targets[touch[i * KP + m]]
                    acc[to] += pieces[m * BS:(m + 1) * BS]
        return carry

    lax.fori_loop(0, GROUP // UNROLL, rows, 0)

    @pl.when(step == MAIN_STEPS - 1)
    def _():
        prev_ref[...] = acc[0:CB].astype(jnp.bfloat16)
        own_ref[...] = acc[CB:2 * CB]
        next_ref[...] = acc[2 * CB:3 * CB].astype(jnp.bfloat16)


def halo_part(codes, touch, targets, p_prev, p_next, part, a_blocks, p_local):
    whole = lambda s, *_: (0, 0, 0)
    rows = (CB, BS, KC * BS)
    return pl.pallas_call(
        halo_kernel,
        grid_spec=pltpu.PrefetchScalarGridSpec(
            num_scalar_prefetch=3,
            grid=(MAIN_STEPS,),
            in_specs=[
                pl.BlockSpec((HALO, BS, KP * BS), whole),
                pl.BlockSpec((HALO, BS, KP * BS), whole),
                pl.BlockSpec((GROUP, BS, KC * BS), lambda s, *_: (s, 0, 0)),
                pl.BlockSpec((GROUP, BS, 2 * BS), lambda s, *_: (s, 0, KA // 2 - 1)),
                pl.BlockSpec((GROUP, BS, KP * BS), lambda s, *_: (s, 0, 0)),
            ],
            out_specs=[pl.BlockSpec(rows, whole)] * 3,
            scratch_shapes=[
                pltpu.VMEM((2 * HALO * SUBSETS, BS, 128), jnp.bfloat16),
                pltpu.VMEM((TARGETS, BS, KC * BS), jnp.float32),
            ],
        ),
        out_shape=[
            jax.ShapeDtypeStruct(rows, jnp.float32),
            jax.ShapeDtypeStruct(rows, jnp.bfloat16),
            jax.ShapeDtypeStruct(rows, jnp.bfloat16),
        ],
        compiler_params=pltpu.CompilerParams(vmem_limit_bytes=54 * 1024 * 1024),
        cost_estimate=pl.CostEstimate(flops=16_000_000_000, bytes_accessed=20_000_000, transcendentals=0),
    )(codes, touch, targets, p_prev, p_next, part, a_blocks, p_local)


def exchange_kernel(n_grp, n_dev, own_hbm, prev_ref, next_ref, out_ref, own_ref, from_prev, from_next, sems_out,
                    sems_in, own_sem):
    own_copy = pltpu.make_async_copy(own_hbm, own_ref, own_sem)
    own_copy.start()
    g = lax.axis_index("grp")
    d = lax.axis_index("dev")
    count = n_grp * n_dev
    position = g * n_dev + d
    after = lax.rem(position + 1, count)
    before = lax.rem(position + count - 1, count)
    after_id = (after // n_dev, lax.rem(after, n_dev))
    before_id = (before // n_dev, lax.rem(before, n_dev))
    up_id = (lax.rem(g + 1, n_grp), d)
    down_id = (lax.rem(g + n_grp - 1, n_grp), d)

    barrier = pltpu.get_barrier_semaphore()
    for other in (after_id, before_id, up_id, down_id):
        pl.semaphore_signal(barrier, inc=1, device_id=other, device_id_type=MESH)
    pl.semaphore_wait(barrier, 4)

    def copy(source, target, kind, r, device):
        return pltpu.make_async_remote_copy(
            src_ref=source, dst_ref=target, send_sem=sems_out.at[kind, r], recv_sem=sems_in.at[kind, r],
            device_id=device, device_id_type=MESH)

    sent = []
    to_after = [copy(next_ref.at[r], from_prev.at[r], 0, r, after_id) for r in range(CB)]
    to_before = [copy(prev_ref.at[r], from_next.at[r], 1, r, before_id) for r in range(CB)]
    for r in range(CB):
        to_after[r].start()
        to_before[r].start()
    own_copy.wait()
    below = lax.rem(g + n_grp - 1, n_grp)
    above = lax.rem(g + 1, n_grp)
    ups, downs, relays = [], [], []

    def relay(r):
        if r < CB // 2:
            ups[r].wait_recv()
            block = below * CB + r
            onward = copy(out_ref.at[block], out_ref.at[block], 4, r, up_id)
        else:
            downs[r].wait_recv()
            block = above * CB + r
            onward = copy(out_ref.at[block], out_ref.at[block], 4, r, down_id)
        onward.start()
        relays.append(onward)

    for r in range(CB):
        to_after[r].wait_recv()
        to_before[r].wait_recv()
        total = own_ref[r] + from_prev[r].astype(jnp.float32) + from_next[r].astype(jnp.float32)
        block = g * CB + r
        out_ref[block] = total.astype(jnp.bfloat16)
        up = copy(out_ref.at[block], out_ref.at[block], 2, r, up_id)
        down = copy(out_ref.at[block], out_ref.at[block], 3, r, down_id)
        up.start()
        down.start()
        ups.append(up)
        downs.append(down)
        if r >= 1:
            relay(r - 1)
    relay(CB - 1)
    for r in range(CB):
        if r < CB // 2:
            downs[r].wait_recv()
        else:
            ups[r].wait_recv()
        relays[r].wait_recv()
        for c in (to_after[r], to_before[r], ups[r], downs[r], relays[r]):
            c.wait_send()


def exchange(own, to_prev, to_next):
    n_grp, n_dev = lax.axis_size("grp"), lax.axis_size("dev")
    rows = (CB, BS, KC * BS)
    return pl.pallas_call(
        functools.partial(exchange_kernel, n_grp, n_dev),
        out_shape=jax.ShapeDtypeStruct((n_grp * CB, BS, KC * BS), jnp.bfloat16),
        in_specs=[pl.BlockSpec(memory_space=pl.ANY)] * 3,
        out_specs=pl.BlockSpec(memory_space=pltpu.VMEM),
        scratch_shapes=[
            pltpu.VMEM(rows, jnp.float32),
            pltpu.VMEM(rows, jnp.bfloat16),
            pltpu.VMEM(rows, jnp.bfloat16),
            pltpu.SemaphoreType.DMA((5, CB)),
            pltpu.SemaphoreType.DMA((5, CB)),
            pltpu.SemaphoreType.DMA,
        ],
        compiler_params=pltpu.CompilerParams(collective_id=0, has_side_effects=True,
                                             vmem_limit_bytes=32 * 1024 * 1024),
    )(own, to_prev, to_next)


def on_device(a_blocks, a_cols, p_blocks, ap_slots, p_touch, owner_dev, owner_row):
    axes = ("grp", "dev")
    position = lax.axis_index(axes)
    count = lax.axis_size(axes)
    up = [(i, (i + 1) % count) for i in range(count)]
    down = [(j, i) for i, j in up]
    p_prev = lax.ppermute(p_blocks[FB - HALO:], axes, up)
    p_next = lax.ppermute(p_blocks[:HALO], axes, down)

    local = a_cols - position * FB
    slots = ap_slots.reshape(FB, KA, KP)
    weights = jnp.int32(1) << jnp.arange(KP, dtype=jnp.int32)
    hits = slots[:, :, :, None] == jnp.arange(KC, dtype=jnp.int32)
    subset = jnp.sum(jnp.where(hits, weights[:, None], 0), axis=2)
    inside = (local >= 0) & (local < FB)
    here = jnp.where((subset == 0) | ~inside[:, :, None], 0, local[:, :, None] * SUBSETS + subset)
    nearby = jnp.where(local < 0, local + HALO, local - FB + HALO)[:, KA - 2:, None]
    there = jnp.where((subset[:, KA - 2:] == 0) | inside[:, KA - 2:, None], 0, nearby * SUBSETS + subset[:, KA - 2:])
    edge = ((position == 0) | (position == count - 1)).astype(jnp.int32).reshape(1)
    targets = (owner_dev[:, 0] - position + 1) * CB + owner_row
    part = local_part(here.reshape(-1), edge, p_blocks, a_blocks)
    own, to_prev, to_next = halo_part(there.reshape(-1), p_touch.reshape(-1), targets, p_prev, p_next, part,
                                      a_blocks, p_blocks)
    return exchange(own, to_prev, to_next)


def solution(mesh):
    placed = (
        P(("grp", "dev"), None, None),
        P(("grp", "dev"), None),
        P(("grp", "dev"), None, None),
        P(("grp", "dev"), None),
        P(("grp", "dev"), None),
        P(("grp", "dev"), None),
        P(("grp", "dev")),
    )
    return jax.shard_map(
        on_device, mesh=mesh, in_specs=placed, out_specs=P("dev", None, None), check_vma=False
    )
```

```python
import functools

import jax
import jax.numpy as jnp
from jax import lax
from jax.experimental import pallas as pl
from jax.experimental.pallas import tpu as pltpu
from jax.sharding import PartitionSpec as P

BS = 64
KA = 8
KP = 4
KC = 8
CB = 8
NT = 224
FB = 128
HALO = 32
SUBSETS = 1 << KP
P_ROWS = 32
LOCAL_STEPS = FB // P_ROWS
GROUP = 16
UNROLL = 8
MAIN_STEPS = FB // GROUP
TARGETS = 3 * CB
MESH = pl.DeviceIdType.MESH


def build_rows(source, base, table, left):
    def row(r, carry):
        p = source[r].astype(jnp.float32)
        single = []
        for pair in range(KP // 2):
            tile = p[:, pair * 128:(pair + 1) * 128]
            turned = pltpu.roll(tile, 64, 1)
            single.append(jnp.where(left, tile, turned))
            single.append(jnp.where(left, turned, tile))
        sums = {0: None}
        at = (base + r) * SUBSETS
        for subset in range(1, SUBSETS):
            low = subset & -subset
            rest = subset ^ low
            value = single[low.bit_length() - 1]
            if rest:
                value = value + sums[rest]
            sums[subset] = value
            table[at + subset] = value.astype(jnp.bfloat16)
        return carry

    lax.fori_loop(0, P_ROWS, row, 0, unroll=4)


def left_half():
    return lax.broadcasted_iota(jnp.int32, (BS, 128), 1) < 64


def coefficients(table, codes, first, blocks, nt, left):
    rows = []
    for k in range(blocks):
        tiles = []
        for s in range(4 * nt, 4 * nt + 4, 2):
            at = (k * KC + s) * FB + first
            tiles.append(jnp.where(left, table[codes[at]], table[codes[at + FB]]))
        rows.append(jnp.concatenate(tiles, axis=1))
    return jnp.concatenate(rows, axis=0)


def local_kernel(codes, edge, p_ref, a_ref, out_ref, table):
    step = pl.program_id(0)
    left = left_half()

    @pl.when(step == 0)
    def _():
        table[0] = jnp.zeros((BS, 128), jnp.bfloat16)

    @pl.when(step < LOCAL_STEPS)
    def _():
        build_rows(p_ref, step * P_ROWS, table, left)

    def assemble(cuts):
        first = (step - LOCAL_STEPS) * GROUP

        def rows(it, carry):
            for u in range(UNROLL):
                r = it * UNROLL + u
                for nt in range(2):
                    total = None
                    for low, high in cuts:
                        weights = coefficients(table, codes, low * KC * FB + first + r, high - low, nt, left)
                        part = jnp.dot(a_ref[r, :, low * BS:high * BS], weights,
                                       preferred_element_type=jnp.float32)
                        total = part if total is None else total + part
                    out_ref[r, :, nt * 256:(nt + 1) * 256] = total.astype(jnp.bfloat16)
            return carry

        lax.fori_loop(0, GROUP // UNROLL, rows, 0)

    @pl.when((step >= LOCAL_STEPS) & (edge[0] == 0))
    def _():
        assemble(((0, 4), (4, KA - 2)))

    @pl.when((step >= LOCAL_STEPS) & (edge[0] != 0))
    def _():
        assemble(((0, 4), (4, KA)))


def local_part(codes, edge, p_local, a_blocks):
    main = lambda s, *_: (jnp.maximum(s - LOCAL_STEPS, 0), 0, 0)
    return pl.pallas_call(
        local_kernel,
        grid_spec=pltpu.PrefetchScalarGridSpec(
            num_scalar_prefetch=2,
            grid=(LOCAL_STEPS + MAIN_STEPS,),
            in_specs=[
                pl.BlockSpec((P_ROWS, BS, KP * BS), lambda s, *_: (jnp.minimum(s, LOCAL_STEPS - 1), 0, 0)),
                pl.BlockSpec((GROUP, BS, KA * BS), main),
            ],
            out_specs=pl.BlockSpec((GROUP, BS, KC * BS), main),
            scratch_shapes=[pltpu.VMEM((FB * SUBSETS, BS, 128), jnp.bfloat16)],
        ),
        out_shape=jax.ShapeDtypeStruct((FB, BS, KC * BS), jnp.bfloat16),
        compiler_params=pltpu.CompilerParams(vmem_limit_bytes=58 * 1024 * 1024),
        cost_estimate=pl.CostEstimate(flops=16_000_000_000, bytes_accessed=20_000_000, transcendentals=0),
    )(codes, edge, p_local, a_blocks)


def halo_kernel(codes, touch, targets, p_prev, p_next, part_ref, a_ref, p_ref, own_ref, prev_ref, next_ref,
                table, acc):
    step = pl.program_id(0)
    left = left_half()

    @pl.when(step == 0)
    def _():
        acc[...] = jnp.zeros_like(acc)
        build_rows(p_prev, 0, table, left)
        build_rows(p_next, HALO, table, left)
        table[0] = jnp.zeros((BS, 128), jnp.bfloat16)

    def rows(it, carry):
        kept = []
        for u in range(UNROLL + 1):
            if u < UNROLL:
                r = it * UNROLL + u
                i = step * GROUP + r
                halves = []
                for nt in range(2):
                    weights = coefficients(table, codes, i, 2, nt, left)
                    total = jnp.dot(a_ref[r], weights, preferred_element_type=jnp.float32)
                    total = total + part_ref[r, :, nt * 256:(nt + 1) * 256].astype(jnp.float32)
                    halves.append(total.astype(jnp.bfloat16))
                kept.append(jnp.concatenate(halves, axis=1))
            if u >= 1:
                r = it * UNROLL + u - 1
                i = step * GROUP + r
                pieces = lax.dot_general(p_ref[r], kept[u - 1], (((0,), (0,)), ((), ())),
                                         preferred_element_type=jnp.float32)
                for m in range(KP):
                    to = targets[touch[m * FB + i]]
                    acc[to] += pieces[m * BS:(m + 1) * BS]
        return carry

    lax.fori_loop(0, GROUP // UNROLL, rows, 0)

    @pl.when(step == MAIN_STEPS - 1)
    def _():
        prev_ref[...] = acc[0:CB].astype(jnp.bfloat16)
        own_ref[...] = acc[CB:2 * CB]
        next_ref[...] = acc[2 * CB:3 * CB].astype(jnp.bfloat16)


def halo_part(codes, touch, targets, p_prev, p_next, part, a_blocks, p_local):
    whole = lambda s, *_: (0, 0, 0)
    rows = (CB, BS, KC * BS)
    return pl.pallas_call(
        halo_kernel,
        grid_spec=pltpu.PrefetchScalarGridSpec(
            num_scalar_prefetch=3,
            grid=(MAIN_STEPS,),
            in_specs=[
                pl.BlockSpec((HALO, BS, KP * BS), whole),
                pl.BlockSpec((HALO, BS, KP * BS), whole),
                pl.BlockSpec((GROUP, BS, KC * BS), lambda s, *_: (s, 0, 0)),
                pl.BlockSpec((GROUP, BS, 2 * BS), lambda s, *_: (s, 0, KA // 2 - 1)),
                pl.BlockSpec((GROUP, BS, KP * BS), lambda s, *_: (s, 0, 0)),
            ],
            out_specs=[pl.BlockSpec(rows, whole)] * 3,
            scratch_shapes=[
                pltpu.VMEM((2 * HALO * SUBSETS, BS, 128), jnp.bfloat16),
                pltpu.VMEM((TARGETS, BS, KC * BS), jnp.float32),
            ],
        ),
        out_shape=[
            jax.ShapeDtypeStruct(rows, jnp.float32),
            jax.ShapeDtypeStruct(rows, jnp.bfloat16),
            jax.ShapeDtypeStruct(rows, jnp.bfloat16),
        ],
        compiler_params=pltpu.CompilerParams(vmem_limit_bytes=49 * 1024 * 1024),
        cost_estimate=pl.CostEstimate(flops=16_000_000_000, bytes_accessed=20_000_000, transcendentals=0),
    )(codes, touch, targets, p_prev, p_next, part, a_blocks, p_local)


def exchange_kernel(n_grp, n_dev, own_hbm, prev_ref, next_ref, out_ref, own_ref, from_prev, from_next, sems_out,
                    sems_in, own_sem):
    own_copy = pltpu.make_async_copy(own_hbm, own_ref, own_sem)
    own_copy.start()
    g = lax.axis_index("grp")
    d = lax.axis_index("dev")
    count = n_grp * n_dev
    position = g * n_dev + d
    after = lax.rem(position + 1, count)
    before = lax.rem(position + count - 1, count)
    after_id = (after // n_dev, lax.rem(after, n_dev))
    before_id = (before // n_dev, lax.rem(before, n_dev))
    up_id = (lax.rem(g + 1, n_grp), d)
    down_id = (lax.rem(g + n_grp - 1, n_grp), d)

    barrier = pltpu.get_barrier_semaphore()
    for other in (after_id, before_id, up_id, down_id):
        pl.semaphore_signal(barrier, inc=1, device_id=other, device_id_type=MESH)
    pl.semaphore_wait(barrier, 4)

    def copy(source, target, kind, r, device):
        return pltpu.make_async_remote_copy(
            src_ref=source, dst_ref=target, send_sem=sems_out.at[kind, r], recv_sem=sems_in.at[kind, r],
            device_id=device, device_id_type=MESH)

    sent = []
    to_after = [copy(next_ref.at[r], from_prev.at[r], 0, r, after_id) for r in range(CB)]
    to_before = [copy(prev_ref.at[r], from_next.at[r], 1, r, before_id) for r in range(CB)]
    for r in range(3):
        to_after[r].start()
        to_before[r].start()
    own_copy.wait()
    below = lax.rem(g + n_grp - 1, n_grp)
    above = lax.rem(g + 1, n_grp)
    ups, downs, relays = [], [], [None] * CB

    def relay(r):
        if r < CB // 2:
            ups[r].wait_recv()
            block = below * CB + r
            onward = copy(out_ref.at[block], out_ref.at[block], 4, r, up_id)
        else:
            downs[r].wait_recv()
            block = above * CB + r
            onward = copy(out_ref.at[block], out_ref.at[block], 4, r, down_id)
        onward.start()
        relays[r] = onward

    for r in range(CB):
        to_after[r].wait_recv()
        to_before[r].wait_recv()
        if r + 3 < CB:
            to_after[r].wait_send()
            to_before[r].wait_send()
            to_after[r + 3].start()
            to_before[r + 3].start()
        total = own_ref[r] + from_prev[r].astype(jnp.float32) + from_next[r].astype(jnp.float32)
        block = g * CB + r
        out_ref[block] = total.astype(jnp.bfloat16)
        up = copy(out_ref.at[block], out_ref.at[block], 2, r, up_id)
        down = copy(out_ref.at[block], out_ref.at[block], 3, r, down_id)
        up.start()
        down.start()
        ups.append(up)
        downs.append(down)
    for r in range(CB):
        relay(r // 2 + (r % 2) * (CB // 2))
    for r in range(CB):
        if r < CB // 2:
            downs[r].wait_recv()
        else:
            ups[r].wait_recv()
        relays[r].wait_recv()
        for c in (ups[r], downs[r], relays[r]):
            c.wait_send()
        if r + 3 >= CB:
            to_after[r].wait_send()
            to_before[r].wait_send()


def exchange(own, to_prev, to_next):
    n_grp, n_dev = lax.axis_size("grp"), lax.axis_size("dev")
    rows = (CB, BS, KC * BS)
    return pl.pallas_call(
        functools.partial(exchange_kernel, n_grp, n_dev),
        out_shape=jax.ShapeDtypeStruct((n_grp * CB, BS, KC * BS), jnp.bfloat16),
        in_specs=[pl.BlockSpec(memory_space=pl.ANY)] * 3,
        out_specs=pl.BlockSpec(memory_space=pltpu.VMEM),
        scratch_shapes=[
            pltpu.VMEM(rows, jnp.float32),
            pltpu.VMEM(rows, jnp.bfloat16),
            pltpu.VMEM(rows, jnp.bfloat16),
            pltpu.SemaphoreType.DMA((5, CB)),
            pltpu.SemaphoreType.DMA((5, CB)),
            pltpu.SemaphoreType.DMA,
        ],
        compiler_params=pltpu.CompilerParams(collective_id=0, has_side_effects=True,
                                             vmem_limit_bytes=32 * 1024 * 1024),
    )(own, to_prev, to_next)


def on_device(a_blocks, a_cols, p_blocks, ap_slots, p_touch, owner_dev, owner_row):
    axes = ("grp", "dev")
    position = lax.axis_index(axes)
    count = lax.axis_size(axes)
    up = [(i, i + 1) for i in range(count - 1)]
    down = [(j, i) for i, j in up]
    p_prev = lax.ppermute(p_blocks[FB - HALO:], axes, up)
    p_next = lax.ppermute(p_blocks[:HALO], axes, down)

    local = a_cols.T - position * FB
    slots = ap_slots.T.reshape(KA, KP, FB)
    weights = jnp.int32(1) << jnp.arange(KP, dtype=jnp.int32)
    hits = slots[:, :, None, :] == jnp.arange(KC, dtype=jnp.int32)[:, None]
    subset = jnp.sum(jnp.where(hits, weights[:, None, None], 0), axis=1)
    inside = (local >= 0) & (local < FB)
    here = jnp.where((subset == 0) | ~inside[:, None, :], 0, local[:, None, :] * SUBSETS + subset)
    nearby = jnp.where(local < 0, local + HALO, local - FB + HALO)[KA - 2:, None, :]
    subset, inside = subset[KA - 2:], inside[KA - 2:, None, :]
    there = jnp.where((subset == 0) | inside, 0, nearby * SUBSETS + subset)
    edge = ((position == 0) | (position == count - 1)).astype(jnp.int32).reshape(1)
    targets = (owner_dev[:, 0] - position + 1) * CB + owner_row
    part = local_part(here.reshape(-1), edge, p_blocks, a_blocks)
    own, to_prev, to_next = halo_part(there.reshape(-1), p_touch.T.reshape(-1), targets, p_prev, p_next, part,
                                      a_blocks, p_blocks)
    return exchange(own, to_prev, to_next)


def solution(mesh):
    placed = (
        P(("grp", "dev"), None, None),
        P(("grp", "dev"), None),
        P(("grp", "dev"), None, None),
        P(("grp", "dev"), None),
        P(("grp", "dev"), None),
        P(("grp", "dev"), None),
        P(("grp", "dev")),
    )
    return jax.shard_map(
        on_device, mesh=mesh, in_specs=placed, out_specs=P("dev", None, None), check_vma=False
    )
```

```python
import functools

import jax
import jax.numpy as jnp
from jax import lax
from jax.experimental import pallas as pl
from jax.experimental.pallas import tpu as pltpu
from jax.sharding import PartitionSpec as P

BS = 64
KA = 8
KP = 4
KC = 8
CB = 8
NT = 224
FB = 128
HALO = 32
SUBSETS = 1 << KP
P_ROWS = 32
LOCAL_STEPS = FB // P_ROWS
GROUP = 16
UNROLL = 8
SEND_STEP = 2
MAIN_STEPS = FB // GROUP
TARGETS = 3 * CB
MESH = pl.DeviceIdType.MESH


def build_rows(source, base, table, left):
    def row(r, carry):
        p = source[r].astype(jnp.float32)
        single = []
        for pair in range(KP // 2):
            tile = p[:, pair * 128:(pair + 1) * 128]
            turned = pltpu.roll(tile, 64, 1)
            single.append(jnp.where(left, tile, turned))
            single.append(jnp.where(left, turned, tile))
        sums = {0: None}
        at = (base + r) * SUBSETS
        for subset in range(1, SUBSETS):
            low = subset & -subset
            rest = subset ^ low
            value = single[low.bit_length() - 1]
            if rest:
                value = value + sums[rest]
            sums[subset] = value
            table[at + subset] = value.astype(jnp.bfloat16)
        return carry

    lax.fori_loop(0, P_ROWS, row, 0, unroll=4)


def left_half():
    return lax.broadcasted_iota(jnp.int32, (BS, 128), 1) < 64


def coefficients(table, codes, first, blocks, nt, left):
    rows = []
    for k in range(blocks):
        tiles = []
        for s in range(4 * nt, 4 * nt + 4, 2):
            at = (k * KC + s) * FB + first
            tiles.append(jnp.where(left, table[codes[at]], table[codes[at + FB]]))
        rows.append(jnp.concatenate(tiles, axis=1))
    return jnp.concatenate(rows, axis=0)


def local_kernel(n_grp, n_dev, codes, p_hbm, p_ref, a_ref, out_ref, prev_out, next_out, table, sems_out,
                 sems_in):
    step = pl.program_id(0)
    left = left_half()
    count = n_grp * n_dev
    position = lax.axis_index("grp") * n_dev + lax.axis_index("dev")
    has_before = position > 0
    has_after = position < count - 1
    after = jnp.minimum(position + 1, count - 1)
    before = jnp.maximum(position - 1, 0)
    after_id = (after // n_dev, lax.rem(after, n_dev))
    before_id = (before // n_dev, lax.rem(before, n_dev))
    barrier = pltpu.get_barrier_semaphore()

    def copy(first, target, kind, device):
        return pltpu.make_async_remote_copy(
            src_ref=p_hbm.at[pl.ds(first, HALO)], dst_ref=target, send_sem=sems_out.at[kind],
            recv_sem=sems_in.at[kind], device_id=device, device_id_type=MESH)

    to_after = copy(FB - HALO, prev_out, 0, after_id)
    to_before = copy(0, next_out, 1, before_id)

    @pl.when((step == 0) & has_before)
    def _():
        pl.semaphore_signal(barrier, inc=1, device_id=before_id, device_id_type=MESH)

    @pl.when((step == 0) & has_after)
    def _():
        pl.semaphore_signal(barrier, inc=1, device_id=after_id, device_id_type=MESH)

    @pl.when((step == SEND_STEP) & has_before & has_after)
    def _():
        pl.semaphore_wait(barrier, 2)
        to_after.start()
        to_before.start()

    @pl.when((step == SEND_STEP) & ~has_before)
    def _():
        pl.semaphore_wait(barrier, 1)
        to_after.start()

    @pl.when((step == SEND_STEP) & ~has_after)
    def _():
        pl.semaphore_wait(barrier, 1)
        to_before.start()

    @pl.when(step == 0)
    def _():
        table[0] = jnp.zeros((BS, 128), jnp.bfloat16)

    @pl.when(step < LOCAL_STEPS)
    def _():
        build_rows(p_ref, step * P_ROWS, table, left)

    def assemble(cuts):
        first = (step - LOCAL_STEPS) * GROUP

        def rows(it, carry):
            for u in range(UNROLL):
                r = it * UNROLL + u
                for nt in range(2):
                    total = None
                    for low, high in cuts:
                        weights = coefficients(table, codes, low * KC * FB + first + r, high - low, nt, left)
                        part = jnp.dot(a_ref[r, :, low * BS:high * BS], weights,
                                       preferred_element_type=jnp.float32)
                        total = part if total is None else total + part
                    out_ref[r, :, nt * 256:(nt + 1) * 256] = total.astype(jnp.bfloat16)
            return carry

        lax.fori_loop(0, GROUP // UNROLL, rows, 0)

    @pl.when((step >= LOCAL_STEPS) & has_before & has_after)
    def _():
        assemble(((0, 4), (4, KA - 2)))

    @pl.when((step >= LOCAL_STEPS) & ~has_before)
    def _():
        assemble(((0, 4), (4, KA - 1)))

    @pl.when((step >= LOCAL_STEPS) & ~has_after)
    def _():
        assemble(((0, 4), (4, KA)))

    last = LOCAL_STEPS + MAIN_STEPS - 1

    @pl.when((step == last) & has_before)
    def _():
        to_after.wait_recv()
        to_before.wait_send()

    @pl.when((step == last) & has_after)
    def _():
        to_before.wait_recv()
        to_after.wait_send()


def local_part(codes, p_local, a_blocks):
    n_grp, n_dev = lax.axis_size("grp"), lax.axis_size("dev")
    halo = jax.ShapeDtypeStruct((HALO, BS, KP * BS), jnp.bfloat16)
    main = lambda s, *_: (jnp.maximum(s - LOCAL_STEPS, 0), 0, 0)
    return pl.pallas_call(
        functools.partial(local_kernel, n_grp, n_dev),
        grid_spec=pltpu.PrefetchScalarGridSpec(
            num_scalar_prefetch=1,
            grid=(LOCAL_STEPS + MAIN_STEPS,),
            in_specs=[
                pl.BlockSpec(memory_space=pl.ANY),
                pl.BlockSpec((P_ROWS, BS, KP * BS), lambda s, *_: (jnp.minimum(s, LOCAL_STEPS - 1), 0, 0)),
                pl.BlockSpec((GROUP, BS, KA * BS), main),
            ],
            out_specs=[
                pl.BlockSpec((GROUP, BS, KC * BS), main),
                pl.BlockSpec(memory_space=pl.ANY),
                pl.BlockSpec(memory_space=pl.ANY),
            ],
            scratch_shapes=[
                pltpu.VMEM((FB * SUBSETS, BS, 128), jnp.bfloat16),
                pltpu.SemaphoreType.DMA((2,)),
                pltpu.SemaphoreType.DMA((2,)),
            ],
        ),
        out_shape=[jax.ShapeDtypeStruct((FB, BS, KC * BS), jnp.bfloat16), halo, halo],
        compiler_params=pltpu.CompilerParams(collective_id=1, has_side_effects=True, vmem_limit_bytes=58 * 1024 * 1024),
        cost_estimate=pl.CostEstimate(flops=16_000_000_000, bytes_accessed=20_000_000, transcendentals=0),
    )(codes, p_local, p_local, a_blocks)


def halo_kernel(codes, touch, targets, edge, p_prev, p_next, part_ref, a_ref, p_ref, own_ref, prev_ref, next_ref,
                table, acc):
    step = pl.program_id(0)
    left = left_half()

    @pl.when(step == 0)
    def _():
        acc[...] = jnp.zeros_like(acc)
        pl.when(edge[0] != 1)(lambda: build_rows(p_prev, 0, table, left))
        pl.when(edge[0] != 2)(lambda: build_rows(p_next, HALO, table, left))
        table[0] = jnp.zeros((BS, 128), jnp.bfloat16)

    def rows(low, high, it, carry):
        kept = []
        for u in range(UNROLL + 1):
            if u < UNROLL:
                r = it * UNROLL + u
                i = step * GROUP + r
                halves = []
                for nt in range(2):
                    weights = coefficients(table, codes, low * KC * FB + i, high - low, nt, left)
                    total = jnp.dot(a_ref[r, :, low * BS:high * BS], weights, preferred_element_type=jnp.float32)
                    total = total + part_ref[r, :, nt * 256:(nt + 1) * 256].astype(jnp.float32)
                    halves.append(total.astype(jnp.bfloat16))
                kept.append(jnp.concatenate(halves, axis=1))
            if u >= 1:
                r = it * UNROLL + u - 1
                i = step * GROUP + r
                pieces = lax.dot_general(p_ref[r], kept[u - 1], (((0,), (0,)), ((), ())),
                                         preferred_element_type=jnp.float32)
                for m in range(KP):
                    to = targets[touch[m * FB + i]]
                    acc[to] += pieces[m * BS:(m + 1) * BS]
        return carry

    for kind, (low, high) in enumerate(((0, 2), (1, 2), (0, 1))):
        @pl.when(edge[0] == kind)
        def _(low=low, high=high):
            lax.fori_loop(0, GROUP // UNROLL, functools.partial(rows, low, high), 0)

    @pl.when(step == MAIN_STEPS - 1)
    def _():
        prev_ref[...] = acc[0:CB].astype(jnp.bfloat16)
        own_ref[...] = acc[CB:2 * CB]
        next_ref[...] = acc[2 * CB:3 * CB].astype(jnp.bfloat16)


def halo_part(codes, touch, targets, edge, p_prev, p_next, part, a_blocks, p_local):
    whole = lambda s, *_: (0, 0, 0)
    rows = (CB, BS, KC * BS)
    return pl.pallas_call(
        halo_kernel,
        grid_spec=pltpu.PrefetchScalarGridSpec(
            num_scalar_prefetch=4,
            grid=(MAIN_STEPS,),
            in_specs=[
                pl.BlockSpec((HALO, BS, KP * BS), whole),
                pl.BlockSpec((HALO, BS, KP * BS), whole),
                pl.BlockSpec((GROUP, BS, KC * BS), lambda s, *_: (s, 0, 0)),
                pl.BlockSpec((GROUP, BS, 2 * BS), lambda s, *_: (s, 0, KA // 2 - 1)),
                pl.BlockSpec((GROUP, BS, KP * BS), lambda s, *_: (s, 0, 0)),
            ],
            out_specs=[pl.BlockSpec(rows, whole)] * 3,
            scratch_shapes=[
                pltpu.VMEM((2 * HALO * SUBSETS, BS, 128), jnp.bfloat16),
                pltpu.VMEM((TARGETS, BS, KC * BS), jnp.float32),
            ],
        ),
        out_shape=[
            jax.ShapeDtypeStruct(rows, jnp.float32),
            jax.ShapeDtypeStruct(rows, jnp.bfloat16),
            jax.ShapeDtypeStruct(rows, jnp.bfloat16),
        ],
        compiler_params=pltpu.CompilerParams(vmem_limit_bytes=49 * 1024 * 1024),
        cost_estimate=pl.CostEstimate(flops=16_000_000_000, bytes_accessed=20_000_000, transcendentals=0),
    )(codes, touch, targets, edge, p_prev, p_next, part, a_blocks, p_local)


def exchange_kernel(n_grp, n_dev, own_hbm, prev_ref, next_ref, out_ref, own_ref, from_prev, from_next, sems_out,
                    sems_in, own_sem):
    own_copy = pltpu.make_async_copy(own_hbm, own_ref, own_sem)
    own_copy.start()
    g = lax.axis_index("grp")
    d = lax.axis_index("dev")
    count = n_grp * n_dev
    position = g * n_dev + d
    after = lax.rem(position + 1, count)
    before = lax.rem(position + count - 1, count)
    after_id = (after // n_dev, lax.rem(after, n_dev))
    before_id = (before // n_dev, lax.rem(before, n_dev))
    up_id = (lax.rem(g + 1, n_grp), d)
    down_id = (lax.rem(g + n_grp - 1, n_grp), d)

    barrier = pltpu.get_barrier_semaphore()
    for other in (after_id, before_id, up_id, down_id):
        pl.semaphore_signal(barrier, inc=1, device_id=other, device_id_type=MESH)
    pl.semaphore_wait(barrier, 4)

    def copy(source, target, kind, r, device):
        return pltpu.make_async_remote_copy(
            src_ref=source, dst_ref=target, send_sem=sems_out.at[kind, r], recv_sem=sems_in.at[kind, r],
            device_id=device, device_id_type=MESH)

    sent = []
    to_after = [copy(next_ref.at[r], from_prev.at[r], 0, r, after_id) for r in range(CB)]
    to_before = [copy(prev_ref.at[r], from_next.at[r], 1, r, before_id) for r in range(CB)]
    for r in range(3):
        to_after[r].start()
        to_before[r].start()
    own_copy.wait()
    below = lax.rem(g + n_grp - 1, n_grp)
    above = lax.rem(g + 1, n_grp)
    ups, downs, relays = [], [], [None] * CB

    def relay(r):
        if r < CB // 2:
            ups[r].wait_recv()
            block = below * CB + r
            onward = copy(out_ref.at[block], out_ref.at[block], 4, r, up_id)
        else:
            downs[r].wait_recv()
            block = above * CB + r
            onward = copy(out_ref.at[block], out_ref.at[block], 4, r, down_id)
        onward.start()
        relays[r] = onward

    for r in range(CB):
        to_after[r].wait_recv()
        to_before[r].wait_recv()
        if r + 3 < CB:
            to_after[r].wait_send()
            to_before[r].wait_send()
            to_after[r + 3].start()
            to_before[r + 3].start()
        total = own_ref[r] + from_prev[r].astype(jnp.float32) + from_next[r].astype(jnp.float32)
        block = g * CB + r
        out_ref[block] = total.astype(jnp.bfloat16)
        up = copy(out_ref.at[block], out_ref.at[block], 2, r, up_id)
        down = copy(out_ref.at[block], out_ref.at[block], 3, r, down_id)
        up.start()
        down.start()
        ups.append(up)
        downs.append(down)
    for r in range(CB):
        relay(r // 2 + (r % 2) * (CB // 2))
    for r in range(CB):
        if r < CB // 2:
            downs[r].wait_recv()
        else:
            ups[r].wait_recv()
        relays[r].wait_recv()
        for c in (ups[r], downs[r], relays[r]):
            c.wait_send()
        if r + 3 >= CB:
            to_after[r].wait_send()
            to_before[r].wait_send()


def exchange(own, to_prev, to_next):
    n_grp, n_dev = lax.axis_size("grp"), lax.axis_size("dev")
    rows = (CB, BS, KC * BS)
    return pl.pallas_call(
        functools.partial(exchange_kernel, n_grp, n_dev),
        out_shape=jax.ShapeDtypeStruct((n_grp * CB, BS, KC * BS), jnp.bfloat16),
        in_specs=[pl.BlockSpec(memory_space=pl.ANY)] * 3,
        out_specs=pl.BlockSpec(memory_space=pltpu.VMEM),
        scratch_shapes=[
            pltpu.VMEM(rows, jnp.float32),
            pltpu.VMEM(rows, jnp.bfloat16),
            pltpu.VMEM(rows, jnp.bfloat16),
            pltpu.SemaphoreType.DMA((5, CB)),
            pltpu.SemaphoreType.DMA((5, CB)),
            pltpu.SemaphoreType.DMA,
        ],
        compiler_params=pltpu.CompilerParams(collective_id=0, has_side_effects=True,
                                             vmem_limit_bytes=32 * 1024 * 1024),
    )(own, to_prev, to_next)


def on_device(a_blocks, a_cols, p_blocks, ap_slots, p_touch, owner_dev, owner_row):
    axes = ("grp", "dev")
    position = lax.axis_index(axes)
    count = lax.axis_size(axes)
    local = a_cols.T - position * FB
    slots = ap_slots.T.reshape(KA, KP, FB)
    weights = jnp.int32(1) << jnp.arange(KP, dtype=jnp.int32)
    hits = slots[:, :, None, :] == jnp.arange(KC, dtype=jnp.int32)[:, None]
    subset = jnp.sum(jnp.where(hits, weights[:, None, None], 0), axis=1)
    inside = (local >= 0) & (local < FB)
    here = jnp.where((subset == 0) | ~inside[:, None, :], 0, local[:, None, :] * SUBSETS + subset)
    nearby = jnp.where(local < 0, local + HALO, local - FB + HALO)[KA - 2:, None, :]
    subset, inside = subset[KA - 2:], inside[KA - 2:, None, :]
    there = jnp.where((subset == 0) | inside, 0, nearby * SUBSETS + subset)
    edge = jnp.where(position == 0, 1, jnp.where(position == count - 1, 2, 0)).astype(jnp.int32).reshape(1)
    targets = (owner_dev[:, 0] - position + 1) * CB + owner_row
    part, p_prev, p_next = local_part(here.reshape(-1), p_blocks, a_blocks)
    own, to_prev, to_next = halo_part(there.reshape(-1), p_touch.T.reshape(-1), targets, edge, p_prev, p_next, part,
                                      a_blocks, p_blocks)
    return exchange(own, to_prev, to_next)


def solution(mesh):
    placed = (
        P(("grp", "dev"), None, None),
        P(("grp", "dev"), None),
        P(("grp", "dev"), None, None),
        P(("grp", "dev"), None),
        P(("grp", "dev"), None),
        P(("grp", "dev"), None),
        P(("grp", "dev")),
    )
    return jax.shard_map(
        on_device, mesh=mesh, in_specs=placed, out_specs=P("dev", None, None), check_vma=False
    )
```

```python
import functools

import jax
import jax.numpy as jnp
from jax import lax
from jax.experimental import pallas as pl
from jax.experimental.pallas import tpu as pltpu
from jax.sharding import PartitionSpec as P

BS = 64
KA = 8
KP = 4
KC = 8
CB = 8
NT = 224
FB = 128
HALO = 32
SUBSETS = 1 << KP
P_ROWS = 32
LOCAL_STEPS = FB // P_ROWS
GROUP = 16
UNROLL = 8
LOCAL_UNROLL = 16
SEND_STEP = 2
MAIN_STEPS = FB // GROUP
TARGETS = 3 * CB
MESH = pl.DeviceIdType.MESH


def build_rows(source, base, table, left):
    def row(r, carry):
        p = source[r].astype(jnp.float32)
        single = []
        for pair in range(KP // 2):
            tile = p[:, pair * 128:(pair + 1) * 128]
            turned = pltpu.roll(tile, 64, 1)
            single.append(jnp.where(left, tile, turned))
            single.append(jnp.where(left, turned, tile))
        sums = {0: None}
        at = (base + r) * SUBSETS
        for subset in range(1, SUBSETS):
            low = subset & -subset
            rest = subset ^ low
            value = single[low.bit_length() - 1]
            if rest:
                value = value + sums[rest]
            sums[subset] = value
            table[at + subset] = value.astype(jnp.bfloat16)
        return carry

    lax.fori_loop(0, P_ROWS, row, 0, unroll=8)


def codes_kernel(place, cols_ref, slots_ref, codes_ref):
    each = lax.broadcasted_iota(jnp.int32, (KC, FB), 0)
    for k in range(KA):
        local = cols_ref[k:k + 1, :] - place[0] * FB
        subset = jnp.zeros((KC, FB), jnp.int32)
        for m in range(KP):
            at = k * KP + m
            subset = subset + jnp.where(slots_ref[at:at + 1, :] == each, 1 << m, 0)
        nearby = jnp.where(local < 0, local + HALO, local - FB + HALO)
        here = (local >= 0) & (local < FB)
        row = jnp.where(here, local, nearby) * SUBSETS + subset
        code = jnp.where(here, row, -row)
        codes_ref[k * KC:(k + 1) * KC, :] = jnp.where(subset == 0, 0, code)


def table_codes(place, cols, slots):
    return pl.pallas_call(
        codes_kernel,
        in_specs=[
            pl.BlockSpec(memory_space=pltpu.SMEM),
            pl.BlockSpec(memory_space=pltpu.VMEM),
            pl.BlockSpec(memory_space=pltpu.VMEM),
        ],
        out_specs=pl.BlockSpec(memory_space=pltpu.VMEM),
        out_shape=jax.ShapeDtypeStruct((KA * KC, FB), jnp.int32),
        compiler_params=pltpu.CompilerParams(vmem_limit_bytes=63 * 1024 * 1024),
    )(place, cols, slots)


def left_half():
    return lax.broadcasted_iota(jnp.int32, (BS, 128), 1) < 64


def coefficients(table, index, low, high, nt, left):
    rows = []
    for k in range(low, high):
        tiles = []
        for s in range(4 * nt, 4 * nt + 4, 2):
            tiles.append(jnp.where(left, table[index(k, s)], table[index(k, s + 1)]))
        rows.append(jnp.concatenate(tiles, axis=1))
    return jnp.concatenate(rows, axis=0)


def local_kernel(n_grp, n_dev, codes, p_hbm, p_ref, a_ref, out_ref, prev_out, next_out, table, sems_out,
                 sems_in):
    step = pl.program_id(0)
    left = left_half()
    count = n_grp * n_dev
    position = lax.axis_index("grp") * n_dev + lax.axis_index("dev")
    has_before = position > 0
    has_after = position < count - 1
    after = jnp.minimum(position + 1, count - 1)
    before = jnp.maximum(position - 1, 0)
    after_id = (after // n_dev, lax.rem(after, n_dev))
    before_id = (before // n_dev, lax.rem(before, n_dev))
    barrier = pltpu.get_barrier_semaphore()

    def copy(first, target, kind, device):
        return pltpu.make_async_remote_copy(
            src_ref=p_hbm.at[pl.ds(first, HALO)], dst_ref=target, send_sem=sems_out.at[kind],
            recv_sem=sems_in.at[kind], device_id=device, device_id_type=MESH)

    to_after = copy(FB - HALO, prev_out, 0, after_id)
    to_before = copy(0, next_out, 1, before_id)

    @pl.when((step == 0) & has_before)
    def _():
        pl.semaphore_signal(barrier, inc=1, device_id=before_id, device_id_type=MESH)

    @pl.when((step == 0) & has_after)
    def _():
        pl.semaphore_signal(barrier, inc=1, device_id=after_id, device_id_type=MESH)

    @pl.when((step == SEND_STEP) & has_before & has_after)
    def _():
        pl.semaphore_wait(barrier, 2)
        to_after.start()
        to_before.start()

    @pl.when((step == SEND_STEP) & ~has_before)
    def _():
        pl.semaphore_wait(barrier, 1)
        to_after.start()

    @pl.when((step == SEND_STEP) & ~has_after)
    def _():
        pl.semaphore_wait(barrier, 1)
        to_before.start()

    @pl.when(step == 0)
    def _():
        table[0] = jnp.zeros((BS, 128), jnp.bfloat16)

    @pl.when(step < LOCAL_STEPS)
    def _():
        build_rows(p_ref, step * P_ROWS, table, left)

    def assemble(cuts):
        first = (step - LOCAL_STEPS) * GROUP

        def rows(it, carry):
            for u in range(LOCAL_UNROLL):
                r = it * LOCAL_UNROLL + u

                def index(k, s, i=first + r):
                    code = codes[(k * KC + s) * FB + i]
                    return code if k < KA - 2 else jnp.maximum(code, 0)

                for nt in range(2):
                    total = None
                    for low, high in cuts:
                        weights = coefficients(table, index, low, high, nt, left)
                        part = jnp.dot(a_ref[r, :, low * BS:high * BS], weights,
                                       preferred_element_type=jnp.float32)
                        total = part if total is None else total + part
                    out_ref[r, :, nt * 256:(nt + 1) * 256] = total.astype(jnp.bfloat16)
            return carry

        lax.fori_loop(0, GROUP // LOCAL_UNROLL, rows, 0)

    @pl.when((step >= LOCAL_STEPS) & has_before & has_after)
    def _():
        assemble(((0, 4), (4, KA - 2)))

    @pl.when((step >= LOCAL_STEPS) & ~has_before)
    def _():
        assemble(((0, 4), (4, KA - 1)))

    @pl.when((step >= LOCAL_STEPS) & ~has_after)
    def _():
        assemble(((0, 4), (4, KA)))

    last = LOCAL_STEPS + MAIN_STEPS - 1

    @pl.when((step == last) & has_before)
    def _():
        to_after.wait_recv()
        to_before.wait_send()

    @pl.when((step == last) & has_after)
    def _():
        to_before.wait_recv()
        to_after.wait_send()


def local_part(codes, p_local, a_blocks):
    n_grp, n_dev = lax.axis_size("grp"), lax.axis_size("dev")
    halo = jax.ShapeDtypeStruct((HALO, BS, KP * BS), jnp.bfloat16)
    main = lambda s, *_: (jnp.maximum(s - LOCAL_STEPS, 0), 0, 0)
    return pl.pallas_call(
        functools.partial(local_kernel, n_grp, n_dev),
        grid_spec=pltpu.PrefetchScalarGridSpec(
            num_scalar_prefetch=1,
            grid=(LOCAL_STEPS + MAIN_STEPS,),
            in_specs=[
                pl.BlockSpec(memory_space=pl.ANY),
                pl.BlockSpec((P_ROWS, BS, KP * BS), lambda s, *_: (jnp.minimum(s, LOCAL_STEPS - 1), 0, 0)),
                pl.BlockSpec((GROUP, BS, KA * BS), main),
            ],
            out_specs=[
                pl.BlockSpec((GROUP, BS, KC * BS), main),
                pl.BlockSpec(memory_space=pl.ANY),
                pl.BlockSpec(memory_space=pl.ANY),
            ],
            scratch_shapes=[
                pltpu.VMEM((FB * SUBSETS, BS, 128), jnp.bfloat16),
                pltpu.SemaphoreType.DMA((2,)),
                pltpu.SemaphoreType.DMA((2,)),
            ],
        ),
        out_shape=[jax.ShapeDtypeStruct((FB, BS, KC * BS), jnp.bfloat16), halo, halo],
        compiler_params=pltpu.CompilerParams(collective_id=1, has_side_effects=True, vmem_limit_bytes=58 * 1024 * 1024),
        cost_estimate=pl.CostEstimate(flops=16_000_000_000, bytes_accessed=20_000_000, transcendentals=0),
    )(codes, p_local, p_local, a_blocks)


def halo_kernel(count, codes, touch, owner_dev, owner_row, place, p_prev, p_next, part_ref, a_ref, p_ref, own_ref, prev_ref, next_ref,
                table, acc):
    step = pl.program_id(0)
    left = left_half()
    position = place[0]
    is_first, is_last = position == 0, position == count - 1

    @pl.when(step == 0)
    def _():
        acc[...] = jnp.zeros_like(acc)
        pl.when(~is_first)(lambda: build_rows(p_prev, 0, table, left))
        pl.when(~is_last)(lambda: build_rows(p_next, HALO, table, left))
        table[0] = jnp.zeros((BS, 128), jnp.bfloat16)

    def rows(low, high, it, carry):
        kept = []
        for u in range(UNROLL + 1):
            if u < UNROLL:
                r = it * UNROLL + u
                i = step * GROUP + r
                halves = []

                def index(k, s, i=i):
                    return jnp.maximum(-codes[((KA - 2 + k) * KC + s) * FB + i], 0)

                for nt in range(2):
                    weights = coefficients(table, index, low, high, nt, left)
                    total = jnp.dot(a_ref[r, :, low * BS:high * BS], weights, preferred_element_type=jnp.float32)
                    total = total + part_ref[r, :, nt * 256:(nt + 1) * 256].astype(jnp.float32)
                    halves.append(total.astype(jnp.bfloat16))
                kept.append(jnp.concatenate(halves, axis=1))
            if u >= 1:
                r = it * UNROLL + u - 1
                i = step * GROUP + r
                pieces = lax.dot_general(p_ref[r], kept[u - 1], (((0,), (0,)), ((), ())),
                                         preferred_element_type=jnp.float32)
                for m in range(KP):
                    t = touch[m * FB + i]
                    to = (owner_dev[t] - position + 1) * CB + owner_row[t]
                    acc[to] += pieces[m * BS:(m + 1) * BS]
        return carry

    for when, low, high in ((~is_first & ~is_last, 0, 2), (is_first, 1, 2), (is_last, 0, 1)):
        @pl.when(when)
        def _(low=low, high=high):
            lax.fori_loop(0, GROUP // UNROLL, functools.partial(rows, low, high), 0)

    @pl.when(step == MAIN_STEPS - 1)
    def _():
        prev_ref[...] = acc[0:CB].astype(jnp.bfloat16)
        own_ref[...] = acc[CB:2 * CB]
        next_ref[...] = acc[2 * CB:3 * CB].astype(jnp.bfloat16)


def halo_part(codes, touch, owner_dev, owner_row, place, p_prev, p_next, part, a_blocks, p_local):
    whole = lambda s, *_: (0, 0, 0)
    rows = (CB, BS, KC * BS)
    return pl.pallas_call(
        functools.partial(halo_kernel, lax.axis_size("grp") * lax.axis_size("dev")),
        grid_spec=pltpu.PrefetchScalarGridSpec(
            num_scalar_prefetch=5,
            grid=(MAIN_STEPS,),
            in_specs=[
                pl.BlockSpec((HALO, BS, KP * BS), whole),
                pl.BlockSpec((HALO, BS, KP * BS), whole),
                pl.BlockSpec((GROUP, BS, KC * BS), lambda s, *_: (s, 0, 0)),
                pl.BlockSpec((GROUP, BS, 2 * BS), lambda s, *_: (s, 0, KA // 2 - 1)),
                pl.BlockSpec((GROUP, BS, KP * BS), lambda s, *_: (s, 0, 0)),
            ],
            out_specs=[pl.BlockSpec(rows, whole)] * 3,
            scratch_shapes=[
                pltpu.VMEM((2 * HALO * SUBSETS, BS, 128), jnp.bfloat16),
                pltpu.VMEM((TARGETS, BS, KC * BS), jnp.float32),
            ],
        ),
        out_shape=[
            jax.ShapeDtypeStruct(rows, jnp.float32),
            jax.ShapeDtypeStruct(rows, jnp.bfloat16),
            jax.ShapeDtypeStruct(rows, jnp.bfloat16),
        ],
        compiler_params=pltpu.CompilerParams(vmem_limit_bytes=51 * 1024 * 1024),
        cost_estimate=pl.CostEstimate(flops=16_000_000_000, bytes_accessed=20_000_000, transcendentals=0),
    )(codes, touch, owner_dev, owner_row, place, p_prev, p_next, part, a_blocks, p_local)


def exchange_kernel(n_grp, n_dev, own_hbm, prev_ref, next_ref, out_ref, own_ref, from_prev, from_next, sems_out,
                    sems_in, own_sem):
    own_copy = pltpu.make_async_copy(own_hbm, own_ref, own_sem)
    own_copy.start()
    g = lax.axis_index("grp")
    d = lax.axis_index("dev")
    count = n_grp * n_dev
    position = g * n_dev + d
    after = lax.rem(position + 1, count)
    before = lax.rem(position + count - 1, count)
    after_id = (after // n_dev, lax.rem(after, n_dev))
    before_id = (before // n_dev, lax.rem(before, n_dev))
    up_id = (lax.rem(g + 1, n_grp), d)
    down_id = (lax.rem(g + n_grp - 1, n_grp), d)

    barrier = pltpu.get_barrier_semaphore()
    for other in (after_id, before_id, up_id, down_id):
        pl.semaphore_signal(barrier, inc=1, device_id=other, device_id_type=MESH)
    pl.semaphore_wait(barrier, 4)

    def copy(source, target, kind, r, device):
        return pltpu.make_async_remote_copy(
            src_ref=source, dst_ref=target, send_sem=sems_out.at[kind, r], recv_sem=sems_in.at[kind, r],
            device_id=device, device_id_type=MESH)

    sent = []
    to_after = [copy(next_ref.at[r], from_prev.at[r], 0, r, after_id) for r in range(CB)]
    to_before = [copy(prev_ref.at[r], from_next.at[r], 1, r, before_id) for r in range(CB)]
    for r in range(3):
        to_after[r].start()
        to_before[r].start()
    own_copy.wait()
    below = lax.rem(g + n_grp - 1, n_grp)
    above = lax.rem(g + 1, n_grp)
    ups, downs, relays = [], [], [None] * CB

    def relay(r):
        if r < CB // 2:
            ups[r].wait_recv()
            block = below * CB + r
            onward = copy(out_ref.at[block], out_ref.at[block], 4, r, up_id)
        else:
            downs[r].wait_recv()
            block = above * CB + r
            onward = copy(out_ref.at[block], out_ref.at[block], 4, r, down_id)
        onward.start()
        relays[r] = onward

    for r in range(CB):
        to_after[r].wait_recv()
        to_before[r].wait_recv()
        if r + 3 < CB:
            to_after[r].wait_send()
            to_before[r].wait_send()
            to_after[r + 3].start()
            to_before[r + 3].start()
        total = own_ref[r] + from_prev[r].astype(jnp.float32) + from_next[r].astype(jnp.float32)
        block = g * CB + r
        out_ref[block] = total.astype(jnp.bfloat16)
        up = copy(out_ref.at[block], out_ref.at[block], 2, r, up_id)
        down = copy(out_ref.at[block], out_ref.at[block], 3, r, down_id)
        up.start()
        down.start()
        ups.append(up)
        downs.append(down)
    for r in range(CB):
        relay(r // 2 + (r % 2) * (CB // 2))
    for r in range(CB):
        if r < CB // 2:
            downs[r].wait_recv()
        else:
            ups[r].wait_recv()
        relays[r].wait_recv()
        for c in (ups[r], downs[r], relays[r]):
            c.wait_send()
        if r + 3 >= CB:
            to_after[r].wait_send()
            to_before[r].wait_send()


def exchange(own, to_prev, to_next):
    n_grp, n_dev = lax.axis_size("grp"), lax.axis_size("dev")
    rows = (CB, BS, KC * BS)
    return pl.pallas_call(
        functools.partial(exchange_kernel, n_grp, n_dev),
        out_shape=jax.ShapeDtypeStruct((n_grp * CB, BS, KC * BS), jnp.bfloat16),
        in_specs=[pl.BlockSpec(memory_space=pl.ANY)] * 3,
        out_specs=pl.BlockSpec(memory_space=pltpu.VMEM),
        scratch_shapes=[
            pltpu.VMEM(rows, jnp.float32),
            pltpu.VMEM(rows, jnp.bfloat16),
            pltpu.VMEM(rows, jnp.bfloat16),
            pltpu.SemaphoreType.DMA((5, CB)),
            pltpu.SemaphoreType.DMA((5, CB)),
            pltpu.SemaphoreType.DMA,
        ],
        compiler_params=pltpu.CompilerParams(collective_id=0, has_side_effects=True,
                                             vmem_limit_bytes=32 * 1024 * 1024),
    )(own, to_prev, to_next)


def on_device(a_blocks, a_cols, p_blocks, ap_slots, p_touch, owner_dev, owner_row):
    axes = ("grp", "dev")
    position = lax.axis_index(axes)
    place = position.astype(jnp.int32).reshape(1)
    codes = table_codes(place, a_cols.T, ap_slots.T).reshape(-1)
    part, p_prev, p_next = local_part(codes, p_blocks, a_blocks)
    own, to_prev, to_next = halo_part(codes, p_touch.T.reshape(-1), owner_dev.reshape(-1), owner_row,
                                      place, p_prev, p_next, part, a_blocks, p_blocks)
    return exchange(own, to_prev, to_next)


def solution(mesh):
    placed = (
        P(("grp", "dev"), None, None),
        P(("grp", "dev"), None),
        P(("grp", "dev"), None, None),
        P(("grp", "dev"), None),
        P(("grp", "dev"), None),
        P(("grp", "dev"), None),
        P(("grp", "dev")),
    )
    return jax.shard_map(
        on_device, mesh=mesh, in_specs=placed, out_specs=P("dev", None, None), check_vma=False
    )
```

```python
import functools

import jax
import jax.numpy as jnp
from jax import lax
from jax.experimental import pallas as pl
from jax.experimental.pallas import tpu as pltpu
from jax.sharding import PartitionSpec as P

BS = 64
KA = 8
KP = 4
KC = 8
CB = 8
NT = 224
FB = 128
HALO = 32
SUBSETS = 1 << KP
P_ROWS = 32
LOCAL_STEPS = FB // P_ROWS
GROUP = 16
LOCAL_UNROLL = 16
HALO_UNROLL = 16
LAG = 2
SEND_STEP = 2
MAIN_STEPS = FB // GROUP
TARGETS = 3 * CB
MESH = pl.DeviceIdType.MESH


def build_rows(source, base, table, left):
    def row(r, carry):
        p = source[r].astype(jnp.float32)
        single = []
        for pair in range(KP // 2):
            tile = p[:, pair * 128:(pair + 1) * 128]
            turned = pltpu.roll(tile, 64, 1)
            single.append(jnp.where(left, tile, turned))
            single.append(jnp.where(left, turned, tile))
        sums = {0: None}
        at = (base + r) * SUBSETS
        for subset in range(1, SUBSETS):
            low = subset & -subset
            rest = subset ^ low
            value = single[low.bit_length() - 1]
            if rest:
                value = value + sums[rest]
            sums[subset] = value
            table[at + subset] = value.astype(jnp.bfloat16)
        return carry

    lax.fori_loop(0, P_ROWS, row, 0, unroll=16)


def codes_kernel(place, cols_ref, slots_ref, codes_ref):
    each = lax.broadcasted_iota(jnp.int32, (KC, FB), 0)
    for k in range(KA):
        local = cols_ref[k:k + 1, :] - place[0] * FB
        subset = jnp.zeros((KC, FB), jnp.int32)
        for m in range(KP):
            at = k * KP + m
            subset = subset + jnp.where(slots_ref[at:at + 1, :] == each, 1 << m, 0)
        nearby = jnp.where(local < 0, local + HALO, local - FB + HALO)
        here = (local >= 0) & (local < FB)
        row = jnp.where(here, local, nearby) * SUBSETS + subset
        code = jnp.where(here, row, -row)
        codes_ref[k * KC:(k + 1) * KC, :] = jnp.where(subset == 0, 0, code)


def table_codes(place, cols, slots):
    return pl.pallas_call(
        codes_kernel,
        in_specs=[
            pl.BlockSpec(memory_space=pltpu.SMEM),
            pl.BlockSpec(memory_space=pltpu.VMEM),
            pl.BlockSpec(memory_space=pltpu.VMEM),
        ],
        out_specs=pl.BlockSpec(memory_space=pltpu.VMEM),
        out_shape=jax.ShapeDtypeStruct((KA * KC, FB), jnp.int32),
        compiler_params=pltpu.CompilerParams(vmem_limit_bytes=63 * 1024 * 1024),
    )(place, cols, slots)


def left_half():
    return lax.broadcasted_iota(jnp.int32, (BS, 128), 1) < 64


def coefficients(table, index, low, high, nt, left):
    rows = []
    for k in range(low, high):
        tiles = []
        for s in range(4 * nt, 4 * nt + 4, 2):
            tiles.append(jnp.where(left, table[index(k, s)], table[index(k, s + 1)]))
        rows.append(jnp.concatenate(tiles, axis=1))
    return jnp.concatenate(rows, axis=0)


def local_kernel(n_grp, n_dev, codes, p_hbm, p_ref, a_ref, out_ref, prev_out, next_out, table, sems_out,
                 sems_in):
    step = pl.program_id(0)
    left = left_half()
    count = n_grp * n_dev
    position = lax.axis_index("grp") * n_dev + lax.axis_index("dev")
    has_before = position > 0
    has_after = position < count - 1
    after = jnp.minimum(position + 1, count - 1)
    before = jnp.maximum(position - 1, 0)
    after_id = (after // n_dev, lax.rem(after, n_dev))
    before_id = (before // n_dev, lax.rem(before, n_dev))
    barrier = pltpu.get_barrier_semaphore()

    def copy(first, target, kind, device):
        return pltpu.make_async_remote_copy(
            src_ref=p_hbm.at[pl.ds(first, HALO)], dst_ref=target, send_sem=sems_out.at[kind],
            recv_sem=sems_in.at[kind], device_id=device, device_id_type=MESH)

    to_after = copy(FB - HALO, prev_out, 0, after_id)
    to_before = copy(0, next_out, 1, before_id)

    @pl.when((step == 0) & has_before)
    def _():
        pl.semaphore_signal(barrier, inc=1, device_id=before_id, device_id_type=MESH)

    @pl.when((step == 0) & has_after)
    def _():
        pl.semaphore_signal(barrier, inc=1, device_id=after_id, device_id_type=MESH)

    @pl.when((step == SEND_STEP) & has_before & has_after)
    def _():
        pl.semaphore_wait(barrier, 2)
        to_after.start()
        to_before.start()

    @pl.when((step == SEND_STEP) & ~has_before)
    def _():
        pl.semaphore_wait(barrier, 1)
        to_after.start()

    @pl.when((step == SEND_STEP) & ~has_after)
    def _():
        pl.semaphore_wait(barrier, 1)
        to_before.start()

    @pl.when(step == 0)
    def _():
        table[0] = jnp.zeros((BS, 128), jnp.bfloat16)

    @pl.when(step < LOCAL_STEPS)
    def _():
        build_rows(p_ref, step * P_ROWS, table, left)

    def assemble(cuts):
        first = (step - LOCAL_STEPS) * GROUP

        def rows(it, carry):
            for u in range(LOCAL_UNROLL):
                r = it * LOCAL_UNROLL + u

                def index(k, s, i=first + r):
                    code = codes[(k * KC + s) * FB + i]
                    return code if k < KA - 2 else jnp.maximum(code, 0)

                for nt in range(2):
                    total = None
                    for low, high in cuts:
                        weights = coefficients(table, index, low, high, nt, left)
                        part = jnp.dot(a_ref[r, :, low * BS:high * BS], weights,
                                       preferred_element_type=jnp.float32)
                        total = part if total is None else total + part
                    out_ref[r, :, nt * 256:(nt + 1) * 256] = total.astype(jnp.bfloat16)
            return carry

        lax.fori_loop(0, GROUP // LOCAL_UNROLL, rows, 0)

    @pl.when((step >= LOCAL_STEPS) & has_before & has_after)
    def _():
        assemble(((0, 4), (4, KA - 2)))

    @pl.when((step >= LOCAL_STEPS) & ~has_before)
    def _():
        assemble(((0, 4), (4, KA - 1)))

    @pl.when((step >= LOCAL_STEPS) & ~has_after)
    def _():
        assemble(((0, 4), (4, KA - 2), (KA - 1, KA)))

    last = LOCAL_STEPS + MAIN_STEPS - 1

    @pl.when((step == last) & has_before)
    def _():
        to_after.wait_recv()
        to_before.wait_send()

    @pl.when((step == last) & has_after)
    def _():
        to_before.wait_recv()
        to_after.wait_send()


def local_part(codes, p_local, a_blocks):
    n_grp, n_dev = lax.axis_size("grp"), lax.axis_size("dev")
    halo = jax.ShapeDtypeStruct((HALO, BS, KP * BS), jnp.bfloat16)
    main = lambda s, *_: (jnp.maximum(s - LOCAL_STEPS, 0), 0, 0)
    return pl.pallas_call(
        functools.partial(local_kernel, n_grp, n_dev),
        grid_spec=pltpu.PrefetchScalarGridSpec(
            num_scalar_prefetch=1,
            grid=(LOCAL_STEPS + MAIN_STEPS,),
            in_specs=[
                pl.BlockSpec(memory_space=pl.ANY),
                pl.BlockSpec((P_ROWS, BS, KP * BS), lambda s, *_: (jnp.minimum(s, LOCAL_STEPS - 1), 0, 0)),
                pl.BlockSpec((GROUP, BS, KA * BS), main),
            ],
            out_specs=[
                pl.BlockSpec((GROUP, BS, KC * BS), main),
                pl.BlockSpec(memory_space=pl.ANY),
                pl.BlockSpec(memory_space=pl.ANY),
            ],
            scratch_shapes=[
                pltpu.VMEM((FB * SUBSETS, BS, 128), jnp.bfloat16),
                pltpu.SemaphoreType.DMA((2,)),
                pltpu.SemaphoreType.DMA((2,)),
            ],
        ),
        out_shape=[jax.ShapeDtypeStruct((FB, BS, KC * BS), jnp.bfloat16), halo, halo],
        compiler_params=pltpu.CompilerParams(collective_id=1, has_side_effects=True, vmem_limit_bytes=58 * 1024 * 1024),
        cost_estimate=pl.CostEstimate(flops=16_000_000_000, bytes_accessed=20_000_000, transcendentals=0),
    )(codes, p_local, p_local, a_blocks)


def halo_kernel(count, codes, touch, owner_dev, owner_row, place, p_prev, p_next, part_ref, a_ref, p_ref, own_ref, prev_ref, next_ref,
                table, acc):
    step = pl.program_id(0)
    left = left_half()
    position = place[0]
    is_first, is_last = position == 0, position == count - 1

    @pl.when(step == 0)
    def _():
        acc[...] = jnp.zeros_like(acc)
        pl.when(~is_first)(lambda: build_rows(p_prev, 0, table, left))
        pl.when(~is_last)(lambda: build_rows(p_next, HALO, table, left))
        table[0] = jnp.zeros((BS, 128), jnp.bfloat16)

    def rows(low, high, it, carry):
        kept = []
        for u in range(HALO_UNROLL + LAG):
            if u < HALO_UNROLL:
                r = it * HALO_UNROLL + u
                i = step * GROUP + r
                halves = []

                def index(k, s, i=i):
                    return jnp.maximum(-codes[((KA - 2 + k) * KC + s) * FB + i], 0)

                for nt in range(2):
                    weights = coefficients(table, index, low, high, nt, left)
                    total = jnp.dot(a_ref[r, :, low * BS:high * BS], weights, preferred_element_type=jnp.float32)
                    total = total + part_ref[r, :, nt * 256:(nt + 1) * 256].astype(jnp.float32)
                    halves.append(total.astype(jnp.bfloat16))
                kept.append(jnp.concatenate(halves, axis=1))
            if u >= LAG:
                r = it * HALO_UNROLL + u - LAG
                i = step * GROUP + r
                pieces = lax.dot_general(p_ref[r], kept[u - LAG], (((0,), (0,)), ((), ())),
                                         preferred_element_type=jnp.float32)
                for m in range(KP):
                    t = touch[m * FB + i]
                    to = (owner_dev[t] - position + 1) * CB + owner_row[t]
                    acc[to] += pieces[m * BS:(m + 1) * BS]
        return carry

    for when, low, high in ((~is_first & ~is_last, 0, 2), (is_first, 1, 2), (is_last, 0, 1)):
        @pl.when(when)
        def _(low=low, high=high):
            lax.fori_loop(0, GROUP // HALO_UNROLL, functools.partial(rows, low, high), 0)

    @pl.when(step == MAIN_STEPS - 1)
    def _():
        prev_ref[...] = acc[0:CB].astype(jnp.bfloat16)
        own_ref[...] = acc[CB:2 * CB]
        next_ref[...] = acc[2 * CB:3 * CB].astype(jnp.bfloat16)


def halo_part(codes, touch, owner_dev, owner_row, place, p_prev, p_next, part, a_blocks, p_local):
    whole = lambda s, *_: (0, 0, 0)
    rows = (CB, BS, KC * BS)
    return pl.pallas_call(
        functools.partial(halo_kernel, lax.axis_size("grp") * lax.axis_size("dev")),
        grid_spec=pltpu.PrefetchScalarGridSpec(
            num_scalar_prefetch=5,
            grid=(MAIN_STEPS,),
            in_specs=[
                pl.BlockSpec((HALO, BS, KP * BS), whole),
                pl.BlockSpec((HALO, BS, KP * BS), whole),
                pl.BlockSpec((GROUP, BS, KC * BS), lambda s, *_: (s, 0, 0)),
                pl.BlockSpec((GROUP, BS, 2 * BS), lambda s, *_: (s, 0, KA // 2 - 1)),
                pl.BlockSpec((GROUP, BS, KP * BS), lambda s, *_: (s, 0, 0)),
            ],
            out_specs=[pl.BlockSpec(rows, whole)] * 3,
            scratch_shapes=[
                pltpu.VMEM((2 * HALO * SUBSETS, BS, 128), jnp.bfloat16),
                pltpu.VMEM((TARGETS, BS, KC * BS), jnp.float32),
            ],
        ),
        out_shape=[
            jax.ShapeDtypeStruct(rows, jnp.float32),
            jax.ShapeDtypeStruct(rows, jnp.bfloat16),
            jax.ShapeDtypeStruct(rows, jnp.bfloat16),
        ],
        compiler_params=pltpu.CompilerParams(vmem_limit_bytes=51 * 1024 * 1024),
        cost_estimate=pl.CostEstimate(flops=16_000_000_000, bytes_accessed=20_000_000, transcendentals=0),
    )(codes, touch, owner_dev, owner_row, place, p_prev, p_next, part, a_blocks, p_local)


def exchange_kernel(n_grp, n_dev, own_hbm, prev_ref, next_ref, out_ref, own_ref, from_prev, from_next, sems_out,
                    sems_in, own_sem):
    own_copy = pltpu.make_async_copy(own_hbm, own_ref, own_sem)
    own_copy.start()
    g = lax.axis_index("grp")
    d = lax.axis_index("dev")
    count = n_grp * n_dev
    position = g * n_dev + d
    after = lax.rem(position + 1, count)
    before = lax.rem(position + count - 1, count)
    after_id = (after // n_dev, lax.rem(after, n_dev))
    before_id = (before // n_dev, lax.rem(before, n_dev))
    up_id = (lax.rem(g + 1, n_grp), d)
    down_id = (lax.rem(g + n_grp - 1, n_grp), d)

    barrier = pltpu.get_barrier_semaphore()
    for other in (after_id, before_id, up_id, down_id):
        pl.semaphore_signal(barrier, inc=1, device_id=other, device_id_type=MESH)
    pl.semaphore_wait(barrier, 4)

    def copy(source, target, kind, r, device):
        return pltpu.make_async_remote_copy(
            src_ref=source, dst_ref=target, send_sem=sems_out.at[kind, r], recv_sem=sems_in.at[kind, r],
            device_id=device, device_id_type=MESH)

    sent = []
    to_after = [copy(next_ref.at[r], from_prev.at[r], 0, r, after_id) for r in range(CB)]
    to_before = [copy(prev_ref.at[r], from_next.at[r], 1, r, before_id) for r in range(CB)]
    for r in range(3):
        to_after[r].start()
        to_before[r].start()
    own_copy.wait()
    below = lax.rem(g + n_grp - 1, n_grp)
    above = lax.rem(g + 1, n_grp)
    ups, downs, relays = [], [], [None] * CB

    def relay(r):
        if r < CB // 2:
            ups[r].wait_recv()
            block = below * CB + r
            onward = copy(out_ref.at[block], out_ref.at[block], 4, r, up_id)
        else:
            downs[r].wait_recv()
            block = above * CB + r
            onward = copy(out_ref.at[block], out_ref.at[block], 4, r, down_id)
        onward.start()
        relays[r] = onward

    for r in range(CB):
        to_after[r].wait_recv()
        to_before[r].wait_recv()
        if r + 3 < CB:
            to_after[r].wait_send()
            to_before[r].wait_send()
            to_after[r + 3].start()
            to_before[r + 3].start()
        total = own_ref[r] + from_prev[r].astype(jnp.float32) + from_next[r].astype(jnp.float32)
        block = g * CB + r
        out_ref[block] = total.astype(jnp.bfloat16)
        up = copy(out_ref.at[block], out_ref.at[block], 2, r, up_id)
        down = copy(out_ref.at[block], out_ref.at[block], 3, r, down_id)
        up.start()
        down.start()
        ups.append(up)
        downs.append(down)
    for r in range(CB):
        relay(r // 2 + (r % 2) * (CB // 2))
    for r in range(CB):
        if r < CB // 2:
            downs[r].wait_recv()
        else:
            ups[r].wait_recv()
        relays[r].wait_recv()
        for c in (ups[r], downs[r], relays[r]):
            c.wait_send()
        if r + 3 >= CB:
            to_after[r].wait_send()
            to_before[r].wait_send()


def exchange(own, to_prev, to_next):
    n_grp, n_dev = lax.axis_size("grp"), lax.axis_size("dev")
    rows = (CB, BS, KC * BS)
    return pl.pallas_call(
        functools.partial(exchange_kernel, n_grp, n_dev),
        out_shape=jax.ShapeDtypeStruct((n_grp * CB, BS, KC * BS), jnp.bfloat16),
        in_specs=[pl.BlockSpec(memory_space=pl.ANY)] * 3,
        out_specs=pl.BlockSpec(memory_space=pltpu.VMEM),
        scratch_shapes=[
            pltpu.VMEM(rows, jnp.float32),
            pltpu.VMEM(rows, jnp.bfloat16),
            pltpu.VMEM(rows, jnp.bfloat16),
            pltpu.SemaphoreType.DMA((5, CB)),
            pltpu.SemaphoreType.DMA((5, CB)),
            pltpu.SemaphoreType.DMA,
        ],
        compiler_params=pltpu.CompilerParams(collective_id=0, has_side_effects=True,
                                             vmem_limit_bytes=32 * 1024 * 1024),
    )(own, to_prev, to_next)


def on_device(a_blocks, a_cols, p_blocks, ap_slots, p_touch, owner_dev, owner_row):
    axes = ("grp", "dev")
    position = lax.axis_index(axes)
    place = position.astype(jnp.int32).reshape(1)
    codes = table_codes(place, a_cols.T, ap_slots.T).reshape(-1)
    part, p_prev, p_next = local_part(codes, p_blocks, a_blocks)
    own, to_prev, to_next = halo_part(codes, p_touch.T.reshape(-1), owner_dev.reshape(-1), owner_row,
                                      place, p_prev, p_next, part, a_blocks, p_blocks)
    return exchange(own, to_prev, to_next)


def solution(mesh):
    placed = (
        P(("grp", "dev"), None, None),
        P(("grp", "dev"), None),
        P(("grp", "dev"), None, None),
        P(("grp", "dev"), None),
        P(("grp", "dev"), None),
        P(("grp", "dev"), None),
        P(("grp", "dev")),
    )
    return jax.shard_map(
        on_device, mesh=mesh, in_specs=placed, out_specs=P("dev", None, None), check_vma=False
    )
```
